512 devices in a mesh: tm: 16 (over z_hi, x, core), space: 32 (over z_lo, y).
Axes of the slice: x: 4, y: 4, z: 16 (z_hi: 2, z_lo: 8; z = z_hi * 8 + z_lo), core: 2. Of those that a mesh axis runs over, the one named last changes fastest.
Arguments:
- initial: float32 [256, 128, 128], P('space'), may hold values from -6 to 6
- guess: float32 [16, 256, 128, 128], P('tm', 'space'), may hold values from -6 to 6
- conductivity: float32 [256, 128, 128], P('space'), may hold values from 0.5 to 2
- source: float32 [256, 128, 128], P('space'), may hold values from -4 to 4
Outputs:
- corrected: float32 [16, 256, 128, 128], P('tm', 'space')
- residual: float32 [16, 256, 128, 128], P('tm', 'space')
The draws below stay inside these ranges and needn't reach their ends.
All inputs are finite; a program needn't handle non-finite values.
Results may differ from the reference program's by a relative error of at most 0.0001.
Values sent between devices are 32-bit elements; how exact they have to be, the bound alone decides.
No kernel may reach another device: no remote copies, remote signals or barrier semaphores. Data moves between devices by JAX's collectives and lax.ppermute only.
A program may use at most 64 MiB of HBM per device.

```python
import math
import jax
import jax.numpy as jnp
from jax import lax

NY = 128
NZ = 128
STEPS = 4
NX = 256
INTERVALS = 16


def levels(stream_key, shape, split, low, top_value):
    def one(position, blocks):
        steps = jax.random.uniform(jax.random.fold_in(jax.random.fold_in(stream_key, 6), position), (blocks,), jnp.float32, low / len(split), top_value / len(split))
        return jnp.repeat(jnp.exp(steps), shape[position] // blocks).reshape((-1,) + (1,) * (len(shape) - position - 1))

    factor_of = one(*split[0])
    for cut in split[1:]:
        factor_of = factor_of * one(*cut)
    return factor_of


def centred(own_key, shape, spread, reach, split=(), dtype=jnp.bfloat16):
    values = spread * jax.random.normal(own_key, shape, jnp.float32)
    if split:
        values = values * levels(own_key, shape, split, -0.22, 0.18)
    return jnp.clip(values, -reach, reach).astype(dtype)


def setup_inputs(seed: int = 0) -> dict:
    arg_keys = jax.random.split(jax.random.key(seed), 5)
    return {
        "initial": centred(arg_keys[0], (NX, NY, NZ), 1.0, 6.0, ((0, 32),), jnp.float32),
        "guess": centred(arg_keys[1], (INTERVALS, NX, NY, NZ), 1.0, 6.0, ((0, 16), (1, 32)), jnp.float32),
        "conductivity": jnp.clip(jnp.exp(math.log(2.0) - 1.3862944 * jax.random.uniform(arg_keys[2], (NX, NY, NZ), jnp.float32) ** levels(arg_keys[2], (NX, NY, NZ), ((0, 32),), -0.2, 0.2)), 0.5, 2.0),
        "source": centred(arg_keys[3], (NX, NY, NZ), 0.5, 4.0, ((0, 32),), jnp.float32),
    }


ALONG_FIRST = 0.1
ALONG_SECOND = 0.1
ALONG_THIRD = 0.0125


def laplace(field_ext, kappa_ext, first_w, second_w, third_w):
    centre = field_ext[1:-1]
    kcentre = kappa_ext[1:-1]
    flux_one = first_w * (0.5 * (kcentre + kappa_ext[2:]) * (field_ext[2:] - centre) - 0.5 * (kcentre + kappa_ext[:-2]) * (centre - field_ext[:-2]))
    side_pad = jnp.pad(centre, ((0, 0), (1, 1), (0, 0)))
    kside_pad = jnp.pad(kcentre, ((0, 0), (1, 1), (0, 0)))
    flux_two = second_w * (0.5 * (kcentre + kside_pad[:, 2:]) * (side_pad[:, 2:] - centre) - 0.5 * (kcentre + kside_pad[:, :-2]) * (centre - side_pad[:, :-2]))
    deep_pad = jnp.pad(centre, ((0, 0), (0, 0), (1, 1)))
    kdeep_pad = jnp.pad(kcentre, ((0, 0), (0, 0), (1, 1)))
    flux_three = third_w * (0.5 * (kcentre + kdeep_pad[:, :, 2:]) * (deep_pad[:, :, 2:] - centre) - 0.5 * (kcentre + kdeep_pad[:, :, :-2]) * (centre - deep_pad[:, :, :-2]))
    return flux_one + flux_two + flux_three


def fine_step(field_ext, kappa_ext, heat):
    return field_ext[1:-1] + laplace(field_ext, kappa_ext, ALONG_FIRST, ALONG_SECOND, ALONG_THIRD) + heat


def pad_first(field):
    return jnp.pad(field, ((1, 1), (0, 0), (0, 0)))


def restrict(field):
    return field.reshape(NX // 2, 2, NY // 2, 2, NZ).mean(axis=(1, 3))


def reference(initial, guess, conductivity, source):
    kappa_pad = pad_first(conductivity)

    def advance(field):
        for repeat in range(STEPS):
            field = fine_step(pad_first(field), kappa_pad, source)
        return field

    def shifted(states):
        return jnp.concatenate([initial[None], states[:-1]], 0)

    first = lax.map(advance, shifted(guess))
    second = lax.map(advance, shifted(first))
    before3 = shifted(second)
    residual = lax.map(advance, before3) - second
    coarse_kappa = restrict(conductivity)
    coarse_pad = pad_first(coarse_kappa)

    def psi(state):
        return state + laplace(pad_first(state), coarse_pad, ALONG_FIRST, ALONG_SECOND, 4.0 * ALONG_THIRD)

    coarse_rhs = lax.map(restrict, residual)
    coarse_now = lax.map(restrict, second)
    coarse_base = lax.map(restrict, before3)
    tau = coarse_rhs + coarse_now - lax.map(psi, coarse_base)

    def link(state, term):
        fresh = term + psi(state)
        return fresh, fresh

    last, states = lax.scan(link, restrict(initial), tau)
    finer = jnp.repeat(jnp.repeat(states - coarse_now, 2, axis=1), 2, axis=2)
    return second + finer, residual
```

```python
import jax
import jax.numpy as jnp
from jax import lax
from jax.sharding import PartitionSpec as P

STEPS = 4
ALONG_FIRST = 0.1
ALONG_SECOND = 0.1
ALONG_THIRD = 0.0125
GROUP = 8


def laplace(field_ext, kappa_ext, first_w, second_w, third_w):
    centre = field_ext[1:-1]
    kcentre = kappa_ext[1:-1]
    flux_one = first_w * (
        0.5 * (kcentre + kappa_ext[2:]) * (field_ext[2:] - centre)
        - 0.5 * (kcentre + kappa_ext[:-2]) * (centre - field_ext[:-2])
    )
    side_pad = jnp.pad(centre, ((0, 0), (1, 1), (0, 0)))
    kside_pad = jnp.pad(kcentre, ((0, 0), (1, 1), (0, 0)))
    flux_two = second_w * (
        0.5 * (kcentre + kside_pad[:, 2:]) * (side_pad[:, 2:] - centre)
        - 0.5 * (kcentre + kside_pad[:, :-2]) * (centre - side_pad[:, :-2])
    )
    deep_pad = jnp.pad(centre, ((0, 0), (0, 0), (1, 1)))
    kdeep_pad = jnp.pad(kcentre, ((0, 0), (0, 0), (1, 1)))
    flux_three = third_w * (
        0.5 * (kcentre + kdeep_pad[:, :, 2:]) * (deep_pad[:, :, 2:] - centre)
        - 0.5 * (kcentre + kdeep_pad[:, :, :-2]) * (centre - deep_pad[:, :, :-2])
    )
    return flux_one + flux_two + flux_three


def per_device(initial, guess, conductivity, source):
    rows, width_two, width_three = conductivity.shape
    crows = rows // 2
    slabs = lax.axis_size("space")
    tm = lax.axis_index("tm")
    sp = lax.axis_index("space")
    local = tm % GROUP
    place = (local + 3) % GROUP

    def cut(array, have, want):
        return array[have - want : array.shape[0] - (have - want)]

    def inside(values, margin, block):
        first = sp * block - margin
        index = first + lax.broadcasted_iota(jnp.int32, (values.shape[0], 1, 1), 0)
        return jnp.where((index >= 0) & (index < slabs * block), values, 0.0)

    def route(block, pairs):
        return lax.ppermute(block, ("tm", "space"), pairs)

    def along_space(block, distance, times=range(2 * GROUP)):
        pairs = [
            (t * slabs + i, t * slabs + i + distance)
            for t in times
            for i in range(slabs)
            if 0 <= i + distance < slabs
        ]
        return route(block, pairs)

    def along_time(block, pairs):
        return lax.ppermute(block, "tm", pairs)

    def ring(shift, groups=(0, 1)):
        return [
            (g * GROUP + i, g * GROUP + (i + shift) % GROUP)
            for g in groups
            for i in range(GROUP)
        ]

    def fine(ext, kappa_wide, source_wide):
        margin = STEPS
        for _ in range(STEPS):
            margin -= 1
            ext = inside(
                ext[1:-1]
                + laplace(
                    ext,
                    cut(kappa_wide, STEPS, margin + 1),
                    ALONG_FIRST,
                    ALONG_SECOND,
                    ALONG_THIRD,
                )
                + cut(source_wide, STEPS - 1, margin),
                margin,
                rows,
            )
        return ext

    def restrict(field):
        return field.reshape(-1, 2, width_two // 2, 2, width_three).mean(axis=(1, 3))

    def coarse(ext, have, steps, kappa_c, kappa_have):
        for _ in range(steps):
            have -= 1
            ext = inside(
                ext[1:-1]
                + laplace(
                    ext,
                    cut(kappa_c, kappa_have, have + 1),
                    ALONG_FIRST,
                    ALONG_SECOND,
                    4.0 * ALONG_THIRD,
                ),
                have,
                crows,
            )
        return ext

    def widen(block, times, margin):
        far = margin - crows
        near = [along_space(block, 1, times), along_space(block, -1, times)]
        ends = [
            along_space(block[crows - far :], 2, times),
            along_space(block[:far], -2, times),
        ]
        return jnp.concatenate([ends[0], near[0], block, near[1], ends[1]], 0)

    current = guess[0]
    crossed = along_time(current, [(6, 14), (7, 15)])
    state = jnp.where(tm == 7, initial, jnp.where(tm >= 14, crossed, current))
    up = along_space(
        jnp.concatenate([state[-STEPS:], conductivity[-STEPS:], source[1 - STEPS :]]), 1
    )
    down = along_space(
        jnp.concatenate([state[:STEPS], conductivity[:STEPS], source[: STEPS - 1]]), -1
    )
    kappa_wide = jnp.concatenate(
        [up[STEPS : 2 * STEPS], conductivity, down[STEPS : 2 * STEPS]], 0
    )
    source_wide = jnp.concatenate([up[2 * STEPS :], source, down[2 * STEPS :]], 0)
    state = fine(
        jnp.concatenate([up[:STEPS], state, down[:STEPS]], 0), kappa_wide, source_wide
    )

    def exchange(field):
        before = along_space(field[-STEPS:], 1)
        after = along_space(field[:STEPS], -1)
        return jnp.concatenate([before, field, after], 0)

    state = jnp.where(tm == 6, initial, state)
    second = fine(exchange(state), kappa_wide, source_wide)
    crossed = along_time(second, [(5, 13)])
    second_home = along_time(second, ring(2))
    state = jnp.where(tm == 5, initial, jnp.where(tm == 13, crossed, second))
    before_third = exchange(state)
    third = fine(before_third, kappa_wide, source_wide)
    third_home = along_time(third, ring(3))

    kappa_c = restrict(kappa_wide)
    base = restrict(before_third[2:-2])
    image = coarse(base, 1, 1, kappa_c, 2)
    tau = restrict(third) - jnp.where(tm == 5, 0.0, image)

    def after(array, mark):
        return lax.optimization_barrier((array, mark))[0]

    low, high = range(GROUP), range(GROUP, 2 * GROUP)
    kappa_own = kappa_c[2:-2]
    tau_wide = widen(jnp.concatenate([tau, kappa_own], 1), low, crows * 2)
    kappa_wide_c = tau_wide[:, width_two // 2 :]
    low_sum = cut(tau_wide[:, : width_two // 2], 8, 7)
    got = along_time(low_sum, ring(4, (0,)))
    got = coarse(got, 7, 4, kappa_wide_c, 8)
    wrapped = jnp.where(place >= 4, 0.0, got)
    low_sum = cut(low_sum, 7, 3) + jnp.where(place >= 4, got, 0.0)
    have = 3
    for shift in (2, 1):
        got = along_time(jnp.stack([low_sum, wrapped]), ring(shift, (0,)))
        ahead = jnp.where(place >= shift, got[0], 0.0)
        around = jnp.where(place >= shift, got[1], got[0])
        ahead = coarse(ahead, have, shift, kappa_wide_c, 8)
        around = coarse(around, have, shift, kappa_wide_c, 8)
        low_sum = cut(low_sum, have, have - shift) + ahead
        wrapped = cut(wrapped, have, have - shift) + around
        have -= shift
    carry = wrapped + coarse(widen(low_sum, low, 8), 8, 8, kappa_wide_c, 8)
    carry_home = along_time(carry, [(i, GROUP + (i + 3) % GROUP) for i in range(GROUP)])
    tau = after(tau, carry)

    tau_wide = widen(jnp.concatenate([tau, kappa_own], 1), high, crows * 2)
    kappa_wide_c = tau_wide[:, width_two // 2 :]
    high_sum = cut(tau_wide[:, : width_two // 2], 8, 7)
    have = 7
    for shift in (4, 2, 1):
        got = along_time(high_sum, ring(shift, (1,)))
        got = coarse(jnp.where(place >= shift, got, 0.0), have, shift, kappa_wide_c, 8)
        high_sum = cut(high_sum, have, have - shift) + got
        have -= shift
    total = jnp.where(tm < GROUP, low_sum, high_sum)
    total_home = along_time(total, ring(3)) + carry_home

    residual = third_home - second_home
    change = total_home - restrict(second_home)
    finer = jnp.repeat(jnp.repeat(change, 2, axis=0), 2, axis=1)
    corrected = second_home + finer
    return (corrected[None], residual[None])


def solution(mesh):
    in_specs = (
        P("space", None, None),
        P("tm", "space", None, None),
        P("space", None, None),
        P("space", None, None),
    )
    out_specs = (P("tm", "space", None, None), P("tm", "space", None, None))
    return jax.shard_map(
        per_device, mesh=mesh, in_specs=in_specs, out_specs=out_specs, check_vma=False
    )
```

```python
import jax
import jax.numpy as jnp
from jax import lax
from jax.sharding import PartitionSpec as P

STEPS = 4
ALONG_FIRST = 0.1
ALONG_SECOND = 0.1
ALONG_THIRD = 0.0125
GROUP = 8


def laplace(field_ext, kappa_ext, first_w, second_w, third_w):
    centre = field_ext[1:-1]
    kcentre = kappa_ext[1:-1]
    flux_one = first_w * (
        0.5 * (kcentre + kappa_ext[2:]) * (field_ext[2:] - centre)
        - 0.5 * (kcentre + kappa_ext[:-2]) * (centre - field_ext[:-2])
    )
    side_pad = jnp.pad(centre, ((0, 0), (1, 1), (0, 0)))
    kside_pad = jnp.pad(kcentre, ((0, 0), (1, 1), (0, 0)))
    flux_two = second_w * (
        0.5 * (kcentre + kside_pad[:, 2:]) * (side_pad[:, 2:] - centre)
        - 0.5 * (kcentre + kside_pad[:, :-2]) * (centre - side_pad[:, :-2])
    )
    deep_pad = jnp.pad(centre, ((0, 0), (0, 0), (1, 1)))
    kdeep_pad = jnp.pad(kcentre, ((0, 0), (0, 0), (1, 1)))
    flux_three = third_w * (
        0.5 * (kcentre + kdeep_pad[:, :, 2:]) * (deep_pad[:, :, 2:] - centre)
        - 0.5 * (kcentre + kdeep_pad[:, :, :-2]) * (centre - deep_pad[:, :, :-2])
    )
    return flux_one + flux_two + flux_three


def per_device(initial, guess, conductivity, source):
    rows, width_two, width_three = conductivity.shape
    crows = rows // 2
    slabs = lax.axis_size("space")
    tm = lax.axis_index("tm")
    sp = lax.axis_index("space")
    local = tm % GROUP
    def cut(array, have, want):
        return array[have - want : array.shape[0] - (have - want)]

    def inside(values, margin, block):
        first = sp * block - margin
        index = first + lax.broadcasted_iota(jnp.int32, (values.shape[0], 1, 1), 0)
        return jnp.where((index >= 0) & (index < slabs * block), values, 0.0)

    def route(block, pairs):
        return lax.ppermute(block, ("tm", "space"), pairs)

    def along_space(block, distance, times=range(2 * GROUP)):
        pairs = [
            (t * slabs + i, t * slabs + i + distance)
            for t in times
            for i in range(slabs)
            if 0 <= i + distance < slabs
        ]
        return route(block, pairs)

    def along_time(block, pairs):
        return lax.ppermute(block, "tm", pairs)

    def ring(shift, groups=(0, 1)):
        return [
            (g * GROUP + i, g * GROUP + (i + shift) % GROUP)
            for g in groups
            for i in range(GROUP)
        ]

    def fine(ext, kappa_wide, source_wide):
        margin = STEPS
        for _ in range(STEPS):
            margin -= 1
            ext = inside(
                ext[1:-1]
                + laplace(
                    ext,
                    cut(kappa_wide, STEPS, margin + 1),
                    ALONG_FIRST,
                    ALONG_SECOND,
                    ALONG_THIRD,
                )
                + cut(source_wide, STEPS - 1, margin),
                margin,
                rows,
            )
        return ext

    def restrict(field):
        return field.reshape(-1, 2, width_two // 2, 2, width_three).mean(axis=(1, 3))

    def coarse(ext, have, steps, kappa_c, kappa_have):
        for _ in range(steps):
            have -= 1
            ext = inside(
                ext[1:-1]
                + laplace(
                    ext,
                    cut(kappa_c, kappa_have, have + 1),
                    ALONG_FIRST,
                    ALONG_SECOND,
                    4.0 * ALONG_THIRD,
                ),
                have,
                crows,
            )
        return ext

    def widen(block, times, margin):
        far = margin - crows
        near = [along_space(block, 1, times), along_space(block, -1, times)]
        ends = [
            along_space(block[crows - far :], 2, times),
            along_space(block[:far], -2, times),
        ]
        return jnp.concatenate([ends[0], near[0], block, near[1], ends[1]], 0)

    def neighbours(block_first, block_last, times=range(2 * GROUP)):
        return along_space(block_last, 1, times), along_space(block_first, -1, times)

    kappa_own = restrict(conductivity)
    state = jnp.where(tm == 15, initial, guess[0])
    up, down = neighbours(
        jnp.concatenate([state[:STEPS], conductivity[:STEPS], source[: STEPS - 1]]),
        jnp.concatenate([state[-STEPS:], conductivity[-STEPS:], source[1 - STEPS :]]),
    )
    kappa_wide = jnp.concatenate(
        [up[STEPS : 2 * STEPS], conductivity, down[STEPS : 2 * STEPS]], 0
    )
    source_wide = jnp.concatenate([up[2 * STEPS :], source, down[2 * STEPS :]], 0)
    state = fine(
        jnp.concatenate([up[:STEPS], state, down[:STEPS]], 0), kappa_wide, source_wide
    )

    state = jnp.where(tm == 14, initial, state)
    packed = kappa_own.reshape(crows // 2, width_two, width_three)
    up, down = neighbours(
        jnp.concatenate([state[:STEPS], packed]),
        jnp.concatenate([state[-STEPS:], packed]),
    )
    shape_c = (crows, width_two // 2, width_three)
    kappa_4 = jnp.concatenate(
        [up[STEPS:].reshape(shape_c), kappa_own, down[STEPS:].reshape(shape_c)], 0
    )
    second = fine(
        jnp.concatenate([up[:STEPS], state, down[:STEPS]], 0), kappa_wide, source_wide
    )

    state = jnp.where(tm == 13, initial, second)
    up, down = neighbours(state[:STEPS], state[-STEPS:])
    second_near = along_time(second, ring(2))
    before_third = jnp.concatenate([up, state, down], 0)
    third = fine(before_third, kappa_wide, source_wide)

    image = coarse(restrict(before_third[2:-2]), 1, 1, kappa_4, 4)
    tau = restrict(third) - jnp.where(tm == 13, 0.0, image)

    up, down = neighbours(tau, tau)
    second_cross = along_time(second_near, [(0, 8), (1, 9), (8, 0), (9, 1)])
    tau_wide = jnp.concatenate([up, tau, down], 0)
    high = tm >= GROUP
    ahead, wrapped = 0.0, 0.0
    got = [along_time(cut(tau_wide, 4, d), ring(d)) for d in (3, 2, 1)]
    third_cross = along_time(third, [(i, i ^ 8) for i in (5, 6, 7, 13, 14, 15)])
    for d, block in zip((3, 2, 1), got):
        apart = high & (local >= 5) & (local < d + 5)
        ahead = ahead + jnp.where((local >= d) & ~apart, block, 0.0)
        wrapped = wrapped + jnp.where(local < d, block, 0.0)
        ahead = coarse(ahead, d, 1, kappa_4, 4)
        wrapped = coarse(wrapped, d, 1, kappa_4, 4)
    ahead = ahead + tau

    both = jnp.stack([ahead, wrapped])

    def diagonal(distance):
        pairs = [
            (t * slabs + i, u * slabs + i + distance)
            for t, u in ring(4)
            for i in range(slabs)
            if 0 <= i + distance < slabs
        ]
        return route(both, pairs)

    got = jnp.concatenate([diagonal(1), diagonal(0), diagonal(-1)], 1)
    more = jnp.where((local >= 4) & ~(high & (local >= 5)), got[0], 0.0)
    behind = jnp.where(local >= 4, got[1], jnp.where(high & (local == 0), 0.0, got[0]))
    ahead = ahead + coarse(more, 4, 4, kappa_4, 4)
    wrapped = wrapped + coarse(behind, 4, 4, kappa_4, 4)

    last = jnp.where(high & (local < 5), 0.0, ahead)
    near = neighbours(last, last)
    two = jnp.concatenate([last, kappa_own], 1)
    far = (along_space(two, 2), along_space(two, -2))
    half = width_two // 2
    last_wide = jnp.concatenate(
        [far[0][:, :half], near[0], last, near[1], far[1][:, :half]], 0
    )
    kappa_8 = jnp.concatenate([far[0][:, half:], kappa_4, far[1][:, half:]], 0)
    carry = wrapped + coarse(last_wide, 8, 8, kappa_8, 8)
    handed = along_time(
        jnp.where(local >= 5, ahead, carry),
        [
            (g * GROUP + i, (1 - g) * GROUP + (i + 3) % GROUP)
            for g in (0, 1)
            for i in range(GROUP)
        ],
    )
    twice = coarse(widen(carry, range(8, 13), 8), 8, 8, kappa_8, 8)
    kept = jnp.where(
        high,
        jnp.where(local < 5, ahead + twice, carry),
        jnp.where(local < 5, ahead, 0.0),
    )
    kept = along_time(kept, ring(3))
    third_home = along_time(jnp.where(local >= 5, third_cross, third), ring(3))
    second_home = jnp.where(local < 2, second_cross, second_near)

    residual = third_home - second_home
    change = handed + kept - restrict(second_home)
    finer = jnp.repeat(jnp.repeat(change, 2, axis=0), 2, axis=1)
    corrected = second_home + finer
    return (corrected[None], residual[None])


def solution(mesh):
    in_specs = (
        P("space", None, None),
        P("tm", "space", None, None),
        P("space", None, None),
        P("space", None, None),
    )
    out_specs = (P("tm", "space", None, None), P("tm", "space", None, None))
    return jax.shard_map(
        per_device, mesh=mesh, in_specs=in_specs, out_specs=out_specs, check_vma=False
    )
```

```python
import functools

import jax
import jax.numpy as jnp
from jax import lax
from jax.experimental import pallas as pl
from jax.experimental.pallas import tpu as pltpu
from jax.sharding import PartitionSpec as P

STEPS = 4
ALONG_FIRST = 0.1
ALONG_SECOND = 0.1
ALONG_THIRD = 0.0125
GROUP = 8
PAD = 8


def lane_mask(shape, *lanes):
    lane = lax.broadcasted_iota(jnp.int32, shape, 1)
    hit = lane == lanes[0]
    for other in lanes[1:]:
        hit = hit | (lane == other)
    return hit


def clear_edges(field):
    rows, wide, depth = field.shape
    zero = jnp.zeros((rows, PAD, depth), jnp.float32)
    field[:, :PAD] = zero
    field[:, wide - PAD :] = zero


def face_weights(kappa, weights, third):
    by_first, by_second, by_third, keep = weights
    rows, wide, depth = kappa.shape
    width = wide - 2 * PAD
    chunk = min(16, width)
    first_w, third_w = 0.5 * ALONG_FIRST, 0.5 * third
    for y in range(PAD, PAD + width, chunk):
        before = kappa[0, y : y + chunk]
        for row in range(rows):
            k = kappa[row, y : y + chunk]
            if row:
                by_first[row, y - PAD : y - PAD + chunk] = first_w * (before + k)
            beside = kappa[row, y - 1 : y - 1 + chunk]
            by_second[row, y : y + chunk] = first_w * (beside + k)
            deeper = pltpu.roll(k, depth - 1, 1)
            by_third[row, y - PAD : y - PAD + chunk] = jnp.where(
                lane_mask(k.shape, depth - 1), 0.0, third_w * (k + deeper)
            )
            keep[row, y - PAD : y - PAD + chunk] = jnp.where(
                lane_mask(k.shape, 0, depth - 1), 1.0 - third_w * k, 1.0
            )
            before = k
    for row in range(rows):
        edge = kappa[row, PAD + width - 1 : 2 * PAD + width - 1]
        by_second[row, PAD + width :] = first_w * edge


def sweep(src, dst, weights, heat, first, count, shift, inside, out=None):
    by_first, by_second, by_third, keep = weights
    wide, depth = src.shape[1:]
    width = wide - 2 * PAD
    chunk = min(16, width)
    for y in range(0, width, chunk):
        here = slice(y + PAD, y + PAD + chunk)
        flat = slice(y, y + chunk)
        v = src[first, here]
        flux = by_first[first + shift, flat] * (v - src[first - 1, here])
        for row in range(first, first + count):
            w = row + shift
            ahead = src[row + 1, here]
            flux_ahead = by_first[w + 1, flat] * (ahead - v)
            up = src[row, y + PAD + 1 : y + PAD + 1 + chunk]
            down = src[row, y + PAD - 1 : y + PAD - 1 + chunk]
            side = by_second[w, y + PAD + 1 : y + PAD + 1 + chunk] * (up - v)
            side = side - by_second[w, here] * (v - down)
            deep = by_third[w, flat] * (pltpu.roll(v, depth - 1, 1) - v)
            deep = deep - pltpu.roll(deep, 1, 1)
            total = keep[w, flat] * v + ((flux_ahead - flux) + side + deep)
            if heat is not None:
                total = total + heat(row, flat)
            mask = inside(row)
            if mask is not None:
                total = total * mask
            if out is None:
                dst[row, here] = total
            else:
                out(row - first, flat, total)
            v, flux = ahead, flux_ahead


def inside_of(place, slabs, margin, block):
    def inside(row):
        if row < margin:
            need = (margin - row + block - 1) // block
            return jnp.where(place >= need, 1.0, 0.0)
        if row >= margin + block:
            need = (row - margin) // block
            return jnp.where(place + need < slabs, 1.0, 0.0)
        return None

    return inside


def fill(field, pieces):
    width = field.shape[1] - 2 * PAD
    for ref, first, count, row in pieces:
        field[row : row + count, PAD : PAD + width] = ref[first : first + count]


def fine_scratch(rows, width, depth):
    high = rows + 2 * STEPS
    padded = pltpu.VMEM((high, width + 2 * PAD, depth), jnp.float32)
    plain = pltpu.VMEM((high, width, depth), jnp.float32)
    return [padded, padded, padded, plain, padded, plain, plain]


def four_steps(where, slabs, up_1, down_1, kappa, source, scratch, out):
    state, other, kappa_wide = scratch[:3]
    weights = scratch[3:7]
    rows = kappa.shape[0]
    for field in (other, kappa_wide):
        clear_edges(field)
    fill(
        kappa_wide,
        [
            (up_1, STEPS, STEPS, 0),
            (kappa, 0, rows, STEPS),
            (down_1, STEPS, STEPS, STEPS + rows),
        ],
    )
    face_weights(kappa_wide, weights, ALONG_THIRD)

    def heat(row, flat):
        if row < STEPS:
            return up_1[2 * STEPS + row - 1, flat]
        if row < STEPS + rows:
            return source[row - STEPS, flat]
        return down_1[2 * STEPS + row - STEPS - rows, flat]

    inside = inside_of(where[1], slabs, STEPS, rows)
    src, dst = state, other
    for step in range(1, STEPS + 1):
        count = rows + 2 * (STEPS - step)
        sweep(
            src, dst, weights, heat, step, count, 0, inside, out if step == STEPS else None
        )
        src, dst = dst, src


def phase_one_kernel(
    slabs, where, up_1, down_1, guess, initial, kappa, source, kappa_c,
    state_out, first_out, last_out, *scratch,
):
    state = scratch[0]
    rows = kappa.shape[0]
    clear_edges(state)
    fill(state, [(up_1, 0, STEPS, 0), (down_1, 0, STEPS, STEPS + rows)])

    @pl.when(where[0] == 15)
    def _():
        fill(state, [(initial, 0, rows, STEPS)])

    @pl.when(where[0] != 15)
    def _():
        fill(state, [(guess, 0, rows, STEPS)])

    def out(row, flat, value):
        state_out[row, flat] = value

    four_steps(where, slabs, up_1, down_1, kappa, source, scratch, out)

    @pl.when(where[0] == 14)
    def _():
        state_out[...] = initial[...]

    first_out[:STEPS] = state_out[:STEPS]
    last_out[:STEPS] = state_out[rows - STEPS :]
    half = kappa_c.shape[1]
    for row in range(rows // 2):
        at = (STEPS + row // 2, slice(row % 2 * half, (row % 2 + 1) * half))
        first_out[at] = kappa_c[row]
        last_out[at] = kappa_c[row]


def phase_two_kernel(
    slabs, where, up_1, down_1, up_2, down_2, before, initial, kappa, source,
    second_out, first_out, last_out, *scratch,
):
    state = scratch[0]
    rows = kappa.shape[0]
    clear_edges(state)
    fill(
        state,
        [
            (up_2, 0, STEPS, 0),
            (before, 0, rows, STEPS),
            (down_2, 0, STEPS, STEPS + rows),
        ],
    )

    def out(row, flat, value):
        second_out[row, flat] = value

    four_steps(where, slabs, up_1, down_1, kappa, source, scratch, out)

    @pl.when(where[0] == 13)
    def _():
        first_out[...] = initial[:STEPS]
        last_out[...] = initial[rows - STEPS :]

    @pl.when(where[0] != 13)
    def _():
        first_out[...] = second_out[:STEPS]
        last_out[...] = second_out[rows - STEPS :]


def coarse_kappa_4(field, up_2, down_2, kappa_c, at):
    block, half = kappa_c.shape[:2]
    clear_edges(field)
    fill(field, [(kappa_c, 0, block, at + block)])
    for row in range(block):
        piece = (STEPS + row // 2, slice(row % 2 * half, (row % 2 + 1) * half))
        field[at + row, PAD : PAD + half] = up_2[piece]
        field[at + 2 * block + row, PAD : PAD + half] = down_2[piece]


def coarse_scratch(rows, width, depth, fields):
    padded = pltpu.VMEM((rows, width + 2 * PAD, depth), jnp.float32)
    plain = pltpu.VMEM((rows, width, depth), jnp.float32)
    return [padded] * fields + [padded, plain, padded, plain, plain]


def phase_three_kernel(
    slabs, where, up_1, down_1, up_2, down_2, up_3, down_3, second, initial, kappa,
    source, kappa_c, third_out, tau_out, *scratch,
):
    state, other = scratch[:2]
    base, spare, kappa_wide, *weights = scratch[7:14]
    pair = scratch[14]
    rows, width = kappa.shape[:2]
    block, half = kappa_c.shape[:2]
    clear_edges(state)
    fill(state, [(up_3, 0, STEPS, 0), (down_3, 0, STEPS, STEPS + rows)])

    @pl.when(where[0] == 13)
    def _():
        fill(state, [(initial, 0, rows, STEPS)])

    @pl.when(where[0] != 13)
    def _():
        fill(state, [(second, 0, rows, STEPS)])

    clear_edges(base)
    for row in range(block + 2):
        fine_row = STEPS - 2 + 2 * row
        pair[...] = (
            state[fine_row, PAD : PAD + width] + state[fine_row + 1, PAD : PAD + width]
        )
        base[row, PAD : PAD + half] = 0.25 * (
            pair[pl.ds(0, half, stride=2), :] + pair[pl.ds(1, half, stride=2), :]
        )

    def out(row, flat, value):
        third_out[row, flat] = value

    four_steps(where, slabs, up_1, down_1, kappa, source, scratch, out)

    coarse_kappa_4(kappa_wide, up_2, down_2, kappa_c, 0)
    face_weights(kappa_wide, weights, 4.0 * ALONG_THIRD)

    def keep(row, flat, value):
        tau_out[row, flat] = value

    sweep(base, spare, weights, None, 1, block, block - 1, lambda row: None, keep)
    use = jnp.where(where[0] == 13, 0.0, 1.0)
    for row in range(block):
        pair[...] = third_out[2 * row] + third_out[2 * row + 1]
        now = 0.25 * (
            pair[pl.ds(0, half, stride=2), :] + pair[pl.ds(1, half, stride=2), :]
        )
        tau_out[row] = now - use * tau_out[row]


def near_sums_kernel(
    slabs, where, got_3, got_2, got_1, tau, up_2, down_2, kappa_c, both_out, *scratch
):
    ahead, wrapped, spare, kappa_wide, *weights = scratch
    block, half = kappa_c.shape[:2]
    local = lax.rem(where[0], GROUP)
    high = where[0] >= GROUP
    for field in (ahead, wrapped, spare):
        clear_edges(field)
    coarse_kappa_4(kappa_wide, up_2, down_2, kappa_c, 0)
    face_weights(kappa_wide, weights, 4.0 * ALONG_THIRD)
    inside = inside_of(where[1], slabs, block, block)
    for is_ahead in (True, False):
        src, dst = (ahead, spare) if is_ahead else (wrapped, spare)
        for distance, got in ((3, got_3), (2, got_2), (1, got_1)):
            apart = high & (local >= 5) & (local < distance + 5)
            use = (local >= distance) & ~apart if is_ahead else local < distance
            use = jnp.where(use, 1.0, 0.0)
            for row in range(block + 2 * distance):
                at = (row + block - distance, slice(PAD, PAD + half))
                value = use * got[row]
                src[at] = value if distance == 3 else src[at] + value
            if distance == 1:

                def out(row, flat, value, is_ahead=is_ahead):
                    if is_ahead:
                        both_out[0, row, flat] = value + tau[row, flat]
                    else:
                        both_out[1, row, flat] = value

            else:
                out = None
            sweep(
                src, dst, weights, None, block - distance + 1, block + 2 * distance - 2,
                0, inside, out,
            )
            src, dst = dst, src


def far_sums_kernel(
    slabs, where, got_up, got, got_down, both, up_2, down_2, kappa_c,
    ahead_out, wrapped_out, last_out, *scratch,
):
    field, spare, kappa_wide, *weights = scratch
    block, half = kappa_c.shape[:2]
    local = lax.rem(where[0], GROUP)
    high = where[0] >= GROUP
    clear_edges(field)
    clear_edges(spare)
    coarse_kappa_4(kappa_wide, up_2, down_2, kappa_c, 0)
    face_weights(kappa_wide, weights, 4.0 * ALONG_THIRD)
    inside = inside_of(where[1], slabs, block, block)
    late = local >= 4
    to_ahead = jnp.where(late & ~(high & (local >= 5)), 1.0, 0.0)
    from_wrapped = jnp.where(late, 1.0, 0.0)
    from_ahead = jnp.where(late | (high & (local == 0)), 0.0, 1.0)
    for index, result in ((0, ahead_out), (1, wrapped_out)):
        for piece, ref in enumerate((got_up, got, got_down)):
            for row in range(block):
                at = (piece * block + row, slice(PAD, PAD + half))
                if index == 0:
                    field[at] = to_ahead * ref[0, row]
                else:
                    field[at] = from_wrapped * ref[1, row] + from_ahead * ref[0, row]

        def out(row, flat, value, index=index, result=result):
            result[row, flat] = value + both[index, row, flat]

        src, dst = field, spare
        for step in range(1, block + 1):
            count = 3 * block - 2 * step
            sweep(
                src, dst, weights, None, step, count, 0, inside,
                out if step == block else None,
            )
            src, dst = dst, src
    hand_wrapped = high & (local < 5)

    @pl.when(hand_wrapped)
    def _():
        last_out[...] = wrapped_out[...]

    @pl.when(jnp.logical_not(hand_wrapped))
    def _():
        last_out[...] = ahead_out[...]


def hand_over_kernel(
    slabs, where, far_up, near_up, last, near_down, far_down, up_2, down_2, kappa_c,
    ahead, wrapped, handed_out, kept_out, *scratch,
):
    field, spare, kappa_wide, *weights = scratch
    block, half = kappa_c.shape[:2]
    local = lax.rem(where[0], GROUP)
    high = where[0] >= GROUP
    clear_edges(field)
    clear_edges(spare)
    coarse_kappa_4(kappa_wide, up_2, down_2, kappa_c, block)
    inner = slice(PAD, PAD + half)
    for row in range(block):
        kappa_wide[row, inner] = far_up[row, half:]
        kappa_wide[4 * block + row, inner] = far_down[row, half:]
        field[row, inner] = far_up[row, :half]
        field[4 * block + row, inner] = far_down[row, :half]
    fill(
        field,
        [
            (near_up, 0, block, block),
            (last, 0, block, 2 * block),
            (near_down, 0, block, 3 * block),
        ],
    )
    face_weights(kappa_wide, weights, 4.0 * ALONG_THIRD)
    inside = inside_of(where[1], slabs, 2 * block, block)
    early = local < 5

    def one(use):
        return jnp.where(use, 1.0, 0.0)

    hand_image = one(early & ~high)
    hand_wrapped = one(early)
    hand_ahead = one(~early)
    keep_image = one(high)
    keep_wrapped = one(high & ~early)
    keep_ahead = one(early)

    def out(row, flat, value):
        a, w = ahead[row, flat], wrapped[row, flat]
        handed_out[row, flat] = hand_image * value + hand_wrapped * w + hand_ahead * a
        kept_out[row, flat] = keep_image * value + keep_wrapped * w + keep_ahead * a

    src, dst = field, spare
    for step in range(1, 2 * block + 1):
        count = 5 * block - 2 * step
        sweep(
            src, dst, weights, None, step, count, 0, inside,
            out if step == 2 * block else None,
        )
        src, dst = dst, src


def call(kernel, slabs, outs, scratch, where, *args):
    vmem = pl.BlockSpec(memory_space=pltpu.VMEM)
    return pl.pallas_call(
        functools.partial(kernel, slabs),
        out_shape=[jax.ShapeDtypeStruct(shape, jnp.float32) for shape in outs],
        in_specs=[pl.BlockSpec(memory_space=pltpu.SMEM)] + [vmem] * len(args),
        out_specs=[vmem] * len(outs),
        scratch_shapes=scratch,
        compiler_params=pltpu.CompilerParams(vmem_limit_bytes=40 * 2**20),
        cost_estimate=pl.CostEstimate(flops=0, bytes_accessed=0, transcendentals=0),
    )(where, *args)


def per_device(initial, guess, conductivity, source):
    rows, width_two, width_three = conductivity.shape
    crows, half = rows // 2, width_two // 2
    slabs = lax.axis_size("space")
    tm = lax.axis_index("tm")
    sp = lax.axis_index("space")
    local = tm % GROUP
    where = jnp.stack([tm, sp]).astype(jnp.int32)

    def cut(array, have, want):
        return array[have - want : array.shape[0] - (have - want)]

    def route(block, pairs):
        return lax.ppermute(block, ("tm", "space"), pairs)

    def along_space(block, distance):
        pairs = [
            (i, i + distance) for i in range(slabs) if 0 <= i + distance < slabs
        ]
        return lax.ppermute(block, "space", pairs)

    def along_time(block, pairs):
        return lax.ppermute(block, "tm", pairs)

    def ring(shift):
        return [
            (g * GROUP + i, g * GROUP + (i + shift) % GROUP)
            for g in (0, 1)
            for i in range(GROUP)
        ]

    def restrict(field):
        return field.reshape(-1, 2, half, 2, width_three).mean(axis=(1, 3))

    def neighbours(block_first, block_last):
        return along_space(block_last, 1), along_space(block_first, -1)

    block_shape = (rows, width_two, width_three)
    coarse_shape = (crows, half, width_three)
    edge_shape = (STEPS, width_two, width_three)
    packed_shape = (STEPS + crows // 2, width_two, width_three)
    scratch = fine_scratch(rows, width_two, width_three)

    kappa_c = restrict(conductivity)
    ends = [
        jnp.where(tm == 15, initial[part], guess[0][part])
        for part in (slice(0, STEPS), slice(rows - STEPS, rows))
    ]
    sides = neighbours(
        jnp.concatenate([ends[0], conductivity[:STEPS], source[: STEPS - 1]]),
        jnp.concatenate([ends[1], conductivity[-STEPS:], source[1 - STEPS :]]),
    )
    state, first, last = call(
        phase_one_kernel, slabs, [block_shape, packed_shape, packed_shape], scratch,
        where, *sides, guess[0], initial, conductivity, source, kappa_c,
    )
    sides_2 = neighbours(first, last)
    second, first, last = call(
        phase_two_kernel, slabs, [block_shape, edge_shape, edge_shape], scratch,
        where, *sides, *sides_2, state, initial, conductivity, source,
    )
    sides_3 = neighbours(first, last)
    second_near = along_time(second, ring(2))
    third, tau = call(
        phase_three_kernel, slabs, [block_shape, coarse_shape],
        scratch
        + coarse_scratch(3 * crows, half, width_three, 2)
        + [pltpu.VMEM((width_two, width_three), jnp.float32)],
        where, *sides, *sides_2, *sides_3, second, initial, conductivity, source, kappa_c,
    )

    up, down = neighbours(tau, tau)
    second_cross = along_time(second_near, [(0, 8), (1, 9), (8, 0), (9, 1)])
    tau_wide = jnp.concatenate([up, tau, down], 0)
    got = [along_time(cut(tau_wide, crows, d), ring(d)) for d in (3, 2, 1)]
    third_cross = along_time(third, [(i, i ^ 8) for i in (5, 6, 7, 13, 14, 15)])
    (both,) = call(
        near_sums_kernel, slabs, [(2,) + coarse_shape],
        coarse_scratch(3 * crows, half, width_three, 3),
        where, *got, tau, *sides_2, kappa_c,
    )

    def diagonal(distance):
        pairs = [
            (t * slabs + i, u * slabs + i + distance)
            for t, u in ring(4)
            for i in range(slabs)
            if 0 <= i + distance < slabs
        ]
        return route(both, pairs)

    got = [diagonal(1), diagonal(0), diagonal(-1)]
    ahead, wrapped, last = call(
        far_sums_kernel, slabs, [coarse_shape] * 3,
        coarse_scratch(3 * crows, half, width_three, 2),
        where, *got, both, *sides_2, kappa_c,
    )

    near = neighbours(last, last)
    two = jnp.concatenate([last, kappa_c], 1)
    far = (along_space(two, 2), along_space(two, -2))
    handed, kept = call(
        hand_over_kernel, slabs, [coarse_shape] * 2,
        coarse_scratch(5 * crows, half, width_three, 2),
        where, far[0], near[0], last, near[1], far[1], *sides_2, kappa_c, ahead, wrapped,
    )
    handed = along_time(
        handed,
        [
            (g * GROUP + i, (1 - g) * GROUP + (i + 3) % GROUP)
            for g in (0, 1)
            for i in range(GROUP)
        ],
    )
    kept = along_time(kept, ring(3))
    third_home = along_time(jnp.where(local >= 5, third_cross, third), ring(3))
    second_home = jnp.where(local < 2, second_cross, second_near)

    residual = third_home - second_home
    change = handed + kept - restrict(second_home)
    finer = jnp.repeat(jnp.repeat(change, 2, axis=0), 2, axis=1)
    corrected = second_home + finer
    return (corrected[None], residual[None])


def solution(mesh):
    in_specs = (
        P("space", None, None),
        P("tm", "space", None, None),
        P("space", None, None),
        P("space", None, None),
    )
    out_specs = (P("tm", "space", None, None), P("tm", "space", None, None))
    return jax.shard_map(
        per_device, mesh=mesh, in_specs=in_specs, out_specs=out_specs, check_vma=False
    )
```

```python
import functools

import jax
import jax.numpy as jnp
from jax import lax
from jax.experimental import pallas as pl
from jax.experimental.pallas import tpu as pltpu
from jax.sharding import PartitionSpec as P

STEPS = 4
ALONG_FIRST = 0.1
ALONG_SECOND = 0.1
ALONG_THIRD = 0.0125
GROUP = 8
PAD = 8


def lane_mask(shape, *lanes):
    lane = lax.broadcasted_iota(jnp.int32, shape, 1)
    hit = lane == lanes[0]
    for other in lanes[1:]:
        hit = hit | (lane == other)
    return hit


def clear_edges(field):
    rows, wide, depth = field.shape
    zero = jnp.zeros((rows, PAD, depth), jnp.float32)
    field[:, :PAD] = zero
    field[:, wide - PAD :] = zero


def face_weights(kappa, weights, third):
    by_first, by_second, by_third, keep = weights
    rows, wide, depth = kappa.shape
    width = wide - 2 * PAD
    first_w, third_w = 0.5 * ALONG_FIRST, 0.5 * third
    inner = slice(PAD, PAD + width)
    for row in range(rows):
        k = kappa[row, inner]
        if row:
            by_first[row] = first_w * (kappa[row - 1, inner] + k)
        by_second[row, inner] = first_w * (kappa[row, PAD - 1 : PAD - 1 + width] + k)
        by_second[row, PAD + width :] = (
            first_w * kappa[row, PAD + width - 1 : 2 * PAD + width - 1]
        )
        deeper = pltpu.roll(k, depth - 1, 1)
        by_third[row] = jnp.where(
            lane_mask(k.shape, depth - 1), 0.0, third_w * (k + deeper)
        )
        keep[row] = jnp.where(lane_mask(k.shape, 0, depth - 1), 1.0 - third_w * k, 1.0)


def sweep(src, dst, weights, heat, first, count, shift, inside, out=None):
    by_first, by_second, by_third, keep = weights
    wide, depth = src.shape[1:]
    width = wide - 2 * PAD
    most = max(1, 256 // width)
    inner = slice(PAD, PAD + width)
    upper = slice(PAD + 1, PAD + 1 + width)
    lower = slice(PAD - 1, PAD - 1 + width)
    row = first
    while row < first + count:
        key, mask = inside(row)
        end = row + 1
        while end < first + count and end - row < most and inside(end)[0] == key:
            end += 1
        here = slice(row, end)
        w = slice(row + shift, end + shift)
        v = src[here, inner]
        total = by_first[row + shift + 1 : end + shift + 1] * (
            src[row + 1 : end + 1, inner] - v
        ) - by_first[w] * (v - src[row - 1 : end - 1, inner])
        total = total + (
            by_second[w, upper] * (src[here, upper] - v)
            - by_second[w, inner] * (v - src[here, lower])
        )
        deep = by_third[w] * (pltpu.roll(v, depth - 1, 2) - v)
        total = keep[w] * v + (total + (deep - pltpu.roll(deep, 1, 2)))
        if heat is not None:
            total = total + heat(row, end)
        if mask is not None:
            total = total * mask
        if out is None:
            dst[here, inner] = total
        else:
            out(slice(row - first, end - first), total)
        row = end


def inside_of(place, slabs, margin, block):
    def inside(row):
        if row < margin:
            need = (margin - row + block - 1) // block
            return -need, jnp.where(place >= need, 1.0, 0.0)
        if row >= margin + block:
            need = (row - margin) // block
            return need, jnp.where(place + need < slabs, 1.0, 0.0)
        return 0, None

    return inside


def fill(field, pieces):
    width = field.shape[1] - 2 * PAD
    for ref, first, count, row in pieces:
        field[row : row + count, PAD : PAD + width] = ref[first : first + count]


def fine_scratch(rows, width, depth):
    high = rows + 2 * STEPS
    padded = pltpu.VMEM((high, width + 2 * PAD, depth), jnp.float32)
    plain = pltpu.VMEM((high, width, depth), jnp.float32)
    return [padded, padded, padded, plain, padded, plain, plain]


def four_steps(where, slabs, up_1, down_1, kappa, source, scratch, out):
    state, other, kappa_wide = scratch[:3]
    weights = scratch[3:7]
    rows = kappa.shape[0]
    for field in (other, kappa_wide):
        clear_edges(field)
    fill(
        kappa_wide,
        [
            (up_1, STEPS, STEPS, 0),
            (kappa, 0, rows, STEPS),
            (down_1, STEPS, STEPS, STEPS + rows),
        ],
    )
    face_weights(kappa_wide, weights, ALONG_THIRD)

    def heat(row, end):
        if row < STEPS:
            return up_1[2 * STEPS + row - 1 : 2 * STEPS + end - 1]
        if row < STEPS + rows:
            return source[row - STEPS : end - STEPS]
        return down_1[STEPS + row - rows : STEPS + end - rows]

    inside = inside_of(where[1], slabs, STEPS, rows)
    src, dst = state, other
    for step in range(1, STEPS + 1):
        count = rows + 2 * (STEPS - step)
        sweep(
            src, dst, weights, heat, step, count, 0, inside, out if step == STEPS else None
        )
        src, dst = dst, src


def phase_one_kernel(
    slabs, where, up_1, down_1, guess, initial, kappa, source, kappa_c,
    state_out, first_out, last_out, *scratch,
):
    state = scratch[0]
    rows = kappa.shape[0]
    clear_edges(state)
    fill(state, [(up_1, 0, STEPS, 0), (down_1, 0, STEPS, STEPS + rows)])

    @pl.when(where[0] == 15)
    def _():
        fill(state, [(initial, 0, rows, STEPS)])

    @pl.when(where[0] != 15)
    def _():
        fill(state, [(guess, 0, rows, STEPS)])

    def out(rows, value):
        state_out[rows] = value

    four_steps(where, slabs, up_1, down_1, kappa, source, scratch, out)

    @pl.when(where[0] == 14)
    def _():
        state_out[...] = initial[...]

    first_out[:STEPS] = state_out[:STEPS]
    last_out[:STEPS] = state_out[rows - STEPS :]
    half = kappa_c.shape[1]
    for row in range(rows // 2):
        at = (STEPS + row // 2, slice(row % 2 * half, (row % 2 + 1) * half))
        first_out[at] = kappa_c[row]
        last_out[at] = kappa_c[row]


def phase_two_kernel(
    slabs, where, up_1, down_1, up_2, down_2, before, initial, kappa, source,
    second_out, first_out, last_out, *scratch,
):
    state = scratch[0]
    rows = kappa.shape[0]
    clear_edges(state)
    fill(
        state,
        [
            (up_2, 0, STEPS, 0),
            (before, 0, rows, STEPS),
            (down_2, 0, STEPS, STEPS + rows),
        ],
    )

    def out(rows, value):
        second_out[rows] = value

    four_steps(where, slabs, up_1, down_1, kappa, source, scratch, out)

    @pl.when(where[0] == 13)
    def _():
        first_out[...] = initial[:STEPS]
        last_out[...] = initial[rows - STEPS :]

    @pl.when(where[0] != 13)
    def _():
        first_out[...] = second_out[:STEPS]
        last_out[...] = second_out[rows - STEPS :]


def coarse_kappa_4(field, up_2, down_2, kappa_c, at):
    block, half = kappa_c.shape[:2]
    clear_edges(field)
    fill(field, [(kappa_c, 0, block, at + block)])
    for row in range(block):
        piece = (STEPS + row // 2, slice(row % 2 * half, (row % 2 + 1) * half))
        field[at + row, PAD : PAD + half] = up_2[piece]
        field[at + 2 * block + row, PAD : PAD + half] = down_2[piece]


def coarse_scratch(rows, width, depth, fields):
    padded = pltpu.VMEM((rows, width + 2 * PAD, depth), jnp.float32)
    plain = pltpu.VMEM((rows, width, depth), jnp.float32)
    return [padded] * fields + [padded, plain, padded, plain, plain]


def phase_three_kernel(
    slabs, where, up_1, down_1, up_2, down_2, up_3, down_3, second, initial, kappa,
    source, kappa_c, third_out, tau_out, *scratch,
):
    state, other = scratch[:2]
    base, spare, kappa_wide, *weights = scratch[7:14]
    pair = scratch[14]
    rows, width = kappa.shape[:2]
    block, half = kappa_c.shape[:2]
    clear_edges(state)
    fill(state, [(up_3, 0, STEPS, 0), (down_3, 0, STEPS, STEPS + rows)])

    @pl.when(where[0] == 13)
    def _():
        fill(state, [(initial, 0, rows, STEPS)])

    @pl.when(where[0] != 13)
    def _():
        fill(state, [(second, 0, rows, STEPS)])

    clear_edges(base)
    for row in range(block + 2):
        fine_row = STEPS - 2 + 2 * row
        pair[...] = (
            state[fine_row, PAD : PAD + width] + state[fine_row + 1, PAD : PAD + width]
        )
        base[row, PAD : PAD + half] = 0.25 * (
            pair[pl.ds(0, half, stride=2), :] + pair[pl.ds(1, half, stride=2), :]
        )

    def out(rows, value):
        third_out[rows] = value

    four_steps(where, slabs, up_1, down_1, kappa, source, scratch, out)

    coarse_kappa_4(kappa_wide, up_2, down_2, kappa_c, 0)
    face_weights(kappa_wide, weights, 4.0 * ALONG_THIRD)

    def keep(rows, value):
        tau_out[rows] = value

    sweep(base, spare, weights, None, 1, block, block - 1, lambda row: (0, None), keep)
    use = jnp.where(where[0] == 13, 0.0, 1.0)
    for row in range(block):
        pair[...] = third_out[2 * row] + third_out[2 * row + 1]
        now = 0.25 * (
            pair[pl.ds(0, half, stride=2), :] + pair[pl.ds(1, half, stride=2), :]
        )
        tau_out[row] = now - use * tau_out[row]


def near_sums_kernel(
    slabs, where, got_3, got_2, got_1, tau, up_2, down_2, kappa_c, both_out, *scratch
):
    ahead, wrapped, spare, kappa_wide, *weights = scratch
    block, half = kappa_c.shape[:2]
    local = lax.rem(where[0], GROUP)
    high = where[0] >= GROUP
    for field in (ahead, wrapped, spare):
        clear_edges(field)
    coarse_kappa_4(kappa_wide, up_2, down_2, kappa_c, 0)
    face_weights(kappa_wide, weights, 4.0 * ALONG_THIRD)
    inside = inside_of(where[1], slabs, block, block)
    for is_ahead in (True, False):
        src, dst = (ahead, spare) if is_ahead else (wrapped, spare)
        for distance, got in ((3, got_3), (2, got_2), (1, got_1)):
            apart = high & (local >= 5) & (local < distance + 5)
            use = (local >= distance) & ~apart if is_ahead else local < distance
            use = jnp.where(use, 1.0, 0.0)
            for row in range(block + 2 * distance):
                at = (row + block - distance, slice(PAD, PAD + half))
                value = use * got[row]
                src[at] = value if distance == 3 else src[at] + value
            if distance == 1:

                def out(rows, value, is_ahead=is_ahead):
                    if is_ahead:
                        both_out[0, rows] = value + tau[rows]
                    else:
                        both_out[1, rows] = value

            else:
                out = None
            sweep(
                src, dst, weights, None, block - distance + 1, block + 2 * distance - 2,
                0, inside, out,
            )
            src, dst = dst, src


def far_sums_kernel(
    slabs, where, got_up, got, got_down, both, up_2, down_2, kappa_c,
    ahead_out, wrapped_out, last_out, *scratch,
):
    field, spare, kappa_wide, *weights = scratch
    block, half = kappa_c.shape[:2]
    local = lax.rem(where[0], GROUP)
    high = where[0] >= GROUP
    clear_edges(field)
    clear_edges(spare)
    coarse_kappa_4(kappa_wide, up_2, down_2, kappa_c, 0)
    face_weights(kappa_wide, weights, 4.0 * ALONG_THIRD)
    inside = inside_of(where[1], slabs, block, block)
    late = local >= 4
    to_ahead = jnp.where(late & ~(high & (local >= 5)), 1.0, 0.0)
    from_wrapped = jnp.where(late, 1.0, 0.0)
    from_ahead = jnp.where(late | (high & (local == 0)), 0.0, 1.0)
    for index, result in ((0, ahead_out), (1, wrapped_out)):
        for piece, ref in enumerate((got_up, got, got_down)):
            for row in range(block):
                at = (piece * block + row, slice(PAD, PAD + half))
                if index == 0:
                    field[at] = to_ahead * ref[0, row]
                else:
                    field[at] = from_wrapped * ref[1, row] + from_ahead * ref[0, row]

        def out(rows, value, index=index, result=result):
            result[rows] = value + both[index, rows]

        src, dst = field, spare
        for step in range(1, block + 1):
            count = 3 * block - 2 * step
            sweep(
                src, dst, weights, None, step, count, 0, inside,
                out if step == block else None,
            )
            src, dst = dst, src
    hand_wrapped = high & (local < 5)

    @pl.when(hand_wrapped)
    def _():
        last_out[...] = wrapped_out[...]

    @pl.when(jnp.logical_not(hand_wrapped))
    def _():
        last_out[...] = ahead_out[...]


def hand_over_kernel(
    slabs, where, far_up, near_up, last, near_down, far_down, up_2, down_2, kappa_c,
    ahead, wrapped, handed_out, kept_out, *scratch,
):
    field, spare, kappa_wide, *weights = scratch
    block, half = kappa_c.shape[:2]
    local = lax.rem(where[0], GROUP)
    high = where[0] >= GROUP
    clear_edges(field)
    clear_edges(spare)
    coarse_kappa_4(kappa_wide, up_2, down_2, kappa_c, block)
    inner = slice(PAD, PAD + half)
    for row in range(block):
        kappa_wide[row, inner] = far_up[row, half:]
        kappa_wide[4 * block + row, inner] = far_down[row, half:]
        field[row, inner] = far_up[row, :half]
        field[4 * block + row, inner] = far_down[row, :half]
    fill(
        field,
        [
            (near_up, 0, block, block),
            (last, 0, block, 2 * block),
            (near_down, 0, block, 3 * block),
        ],
    )
    face_weights(kappa_wide, weights, 4.0 * ALONG_THIRD)
    inside = inside_of(where[1], slabs, 2 * block, block)
    early = local < 5

    def one(use):
        return jnp.where(use, 1.0, 0.0)

    hand_image = one(early & ~high)
    hand_wrapped = one(early)
    hand_ahead = one(~early)
    keep_image = one(high)
    keep_wrapped = one(high & ~early)
    keep_ahead = one(early)

    def out(rows, value):
        a, w = ahead[rows], wrapped[rows]
        handed_out[rows] = hand_image * value + hand_wrapped * w + hand_ahead * a
        kept_out[rows] = keep_image * value + keep_wrapped * w + keep_ahead * a

    src, dst = field, spare
    for step in range(1, 2 * block + 1):
        count = 5 * block - 2 * step
        sweep(
            src, dst, weights, None, step, count, 0, inside,
            out if step == 2 * block else None,
        )
        src, dst = dst, src


def call(kernel, slabs, outs, scratch, where, *args):
    vmem = pl.BlockSpec(memory_space=pltpu.VMEM)
    return pl.pallas_call(
        functools.partial(kernel, slabs),
        out_shape=[jax.ShapeDtypeStruct(shape, jnp.float32) for shape in outs],
        in_specs=[pl.BlockSpec(memory_space=pltpu.SMEM)] + [vmem] * len(args),
        out_specs=[vmem] * len(outs),
        scratch_shapes=scratch,
        compiler_params=pltpu.CompilerParams(vmem_limit_bytes=40 * 2**20),
        cost_estimate=pl.CostEstimate(flops=0, bytes_accessed=0, transcendentals=0),
    )(where, *args)


def per_device(initial, guess, conductivity, source):
    rows, width_two, width_three = conductivity.shape
    crows, half = rows // 2, width_two // 2
    slabs = lax.axis_size("space")
    tm = lax.axis_index("tm")
    sp = lax.axis_index("space")
    local = tm % GROUP
    where = jnp.stack([tm, sp]).astype(jnp.int32)

    def cut(array, have, want):
        return array[have - want : array.shape[0] - (have - want)]

    def route(block, pairs):
        return lax.ppermute(block, ("tm", "space"), pairs)

    def along_space(block, distance):
        pairs = [
            (i, i + distance) for i in range(slabs) if 0 <= i + distance < slabs
        ]
        return lax.ppermute(block, "space", pairs)

    def along_time(block, pairs):
        return lax.ppermute(block, "tm", pairs)

    def ring(shift):
        return [
            (g * GROUP + i, g * GROUP + (i + shift) % GROUP)
            for g in (0, 1)
            for i in range(GROUP)
        ]

    def restrict(field):
        return field.reshape(-1, 2, half, 2, width_three).mean(axis=(1, 3))

    def neighbours(block_first, block_last):
        return along_space(block_last, 1), along_space(block_first, -1)

    block_shape = (rows, width_two, width_three)
    coarse_shape = (crows, half, width_three)
    edge_shape = (STEPS, width_two, width_three)
    packed_shape = (STEPS + crows // 2, width_two, width_three)
    scratch = fine_scratch(rows, width_two, width_three)

    kappa_c = restrict(conductivity)
    ends = [
        jnp.where(tm == 15, initial[part], guess[0][part])
        for part in (slice(0, STEPS), slice(rows - STEPS, rows))
    ]
    sides = neighbours(
        jnp.concatenate([ends[0], conductivity[:STEPS], source[: STEPS - 1]]),
        jnp.concatenate([ends[1], conductivity[-STEPS:], source[1 - STEPS :]]),
    )
    state, first, last = call(
        phase_one_kernel, slabs, [block_shape, packed_shape, packed_shape], scratch,
        where, *sides, guess[0], initial, conductivity, source, kappa_c,
    )
    sides_2 = neighbours(first, last)
    second, first, last = call(
        phase_two_kernel, slabs, [block_shape, edge_shape, edge_shape], scratch,
        where, *sides, *sides_2, state, initial, conductivity, source,
    )
    sides_3 = neighbours(first, last)
    second_far = along_time(second, [(6, 8), (7, 9), (14, 0), (15, 1)])
    third, tau = call(
        phase_three_kernel, slabs, [block_shape, coarse_shape],
        scratch
        + coarse_scratch(3 * crows, half, width_three, 2)
        + [pltpu.VMEM((width_two, width_three), jnp.float32)],
        where, *sides, *sides_2, *sides_3, second, initial, conductivity, source, kappa_c,
    )

    up, down = neighbours(tau, tau)
    tau_wide = jnp.concatenate([up, tau, down], 0)
    got = [along_time(cut(tau_wide, crows, d), ring(d)) for d in (3, 2, 1)]
    third_near = along_time(third, ring(3))
    third_far = along_time(third_near, [(i, i ^ GROUP) for i in (0, 1, 2, 8, 9, 10)])
    (both,) = call(
        near_sums_kernel, slabs, [(2,) + coarse_shape],
        coarse_scratch(3 * crows, half, width_three, 3),
        where, *got, tau, *sides_2, kappa_c,
    )

    def diagonal(distance):
        pairs = [
            (t * slabs + i, u * slabs + i + distance)
            for t, u in ring(4)
            for i in range(slabs)
            if 0 <= i + distance < slabs
        ]
        return route(both, pairs)

    got = [diagonal(1), diagonal(0), diagonal(-1)]
    ahead, wrapped, last = call(
        far_sums_kernel, slabs, [coarse_shape] * 3,
        coarse_scratch(3 * crows, half, width_three, 2),
        where, *got, both, *sides_2, kappa_c,
    )

    near = neighbours(last, last)
    two = jnp.concatenate([last, kappa_c], 1)
    far = (along_space(two, 2), along_space(two, -2))
    handed, kept = call(
        hand_over_kernel, slabs, [coarse_shape] * 2,
        coarse_scratch(5 * crows, half, width_three, 2),
        where, far[0], near[0], last, near[1], far[1], *sides_2, kappa_c, ahead, wrapped,
    )
    handed = along_time(
        handed,
        [
            (g * GROUP + i, (1 - g) * GROUP + (i + 3) % GROUP)
            for g in (0, 1)
            for i in range(GROUP)
        ],
    )
    kept = along_time(kept, ring(3))
    second_far, third_far = lax.optimization_barrier((second_far, third_far, kept))[:2]
    second_near = along_time(second, ring(2))
    third_home = jnp.where(local < 3, third_far, third_near)
    second_home = jnp.where(local < 2, second_far, second_near)

    residual = third_home - second_home
    change = handed + kept - restrict(second_home)
    finer = jnp.repeat(jnp.repeat(change, 2, axis=0), 2, axis=1)
    corrected = second_home + finer
    return (corrected[None], residual[None])


def solution(mesh):
    in_specs = (
        P("space", None, None),
        P("tm", "space", None, None),
        P("space", None, None),
        P("space", None, None),
    )
    out_specs = (P("tm", "space", None, None), P("tm", "space", None, None))
    return jax.shard_map(
        per_device, mesh=mesh, in_specs=in_specs, out_specs=out_specs, check_vma=False
    )
```

```python
import functools

import jax
import jax.numpy as jnp
from jax import lax
from jax.experimental import pallas as pl
from jax.experimental.pallas import tpu as pltpu
from jax.sharding import PartitionSpec as P

STEPS = 4
ALONG_FIRST = 0.1
ALONG_SECOND = 0.1
ALONG_THIRD = 0.0125
GROUP = 8
PAD = 8


def lane_mask(shape, *lanes):
    lane = lax.broadcasted_iota(jnp.int32, shape, 1)
    hit = lane == lanes[0]
    for other in lanes[1:]:
        hit = hit | (lane == other)
    return hit


def clear_edges(field):
    rows, wide, depth = field.shape
    zero = jnp.zeros((rows, PAD, depth), jnp.float32)
    field[:, :PAD] = zero
    field[:, wide - PAD :] = zero


def face_weights(kappa, weights, third):
    by_first, by_second, by_third, keep = weights
    rows, wide, depth = kappa.shape
    width = wide - 2 * PAD
    first_w, third_w = 0.5 * ALONG_FIRST, 0.5 * third
    inner = slice(PAD, PAD + width)
    for row in range(rows):
        k = kappa[row, inner]
        if row:
            by_first[row] = first_w * (kappa[row - 1, inner] + k)
        by_second[row, inner] = first_w * (kappa[row, PAD - 1 : PAD - 1 + width] + k)
        by_second[row, PAD + width :] = (
            first_w * kappa[row, PAD + width - 1 : 2 * PAD + width - 1]
        )
        deeper = pltpu.roll(k, depth - 1, 1)
        by_third[row] = jnp.where(
            lane_mask(k.shape, depth - 1), 0.0, third_w * (k + deeper)
        )
        keep[row] = jnp.where(lane_mask(k.shape, 0, depth - 1), 1.0 - third_w * k, 1.0)


def sweep(src, dst, weights, heat, first, count, shift, inside, out=None):
    by_first, by_second, by_third, keep = weights
    wide, depth = src.shape[1:]
    width = wide - 2 * PAD
    most = max(1, 256 // width)
    inner = slice(PAD, PAD + width)
    upper = slice(PAD + 1, PAD + 1 + width)
    lower = slice(PAD - 1, PAD - 1 + width)
    row = first
    while row < first + count:
        key, mask = inside(row)
        end = row + 1
        while end < first + count and end - row < most and inside(end)[0] == key:
            end += 1
        here = slice(row, end)
        w = slice(row + shift, end + shift)
        v = src[here, inner]
        total = by_first[row + shift + 1 : end + shift + 1] * (
            src[row + 1 : end + 1, inner] - v
        ) - by_first[w] * (v - src[row - 1 : end - 1, inner])
        total = total + (
            by_second[w, upper] * (src[here, upper] - v)
            - by_second[w, inner] * (v - src[here, lower])
        )
        deep = by_third[w] * (pltpu.roll(v, depth - 1, 2) - v)
        total = keep[w] * v + (total + (deep - pltpu.roll(deep, 1, 2)))
        if heat is not None:
            total = total + heat(row, end)
        if mask is not None:
            total = total * mask
        if out is None:
            dst[here, inner] = total
        else:
            out(slice(row - first, end - first), total)
        row = end


def inside_of(place, slabs, margin, block):
    def inside(row):
        if row < margin:
            need = (margin - row + block - 1) // block
            return -need, jnp.where(place >= need, 1.0, 0.0)
        if row >= margin + block:
            need = (row - margin) // block
            return need, jnp.where(place + need < slabs, 1.0, 0.0)
        return 0, None

    return inside


def fill(field, pieces):
    width = field.shape[1] - 2 * PAD
    for ref, first, count, row in pieces:
        field[row : row + count, PAD : PAD + width] = ref[first : first + count]


def fine_scratch(rows, width, depth):
    high = rows + 2 * STEPS
    padded = pltpu.VMEM((high, width + 2 * PAD, depth), jnp.float32)
    plain = pltpu.VMEM((high, width, depth), jnp.float32)
    return [padded, padded, padded, plain, padded, plain, plain]


def four_steps(where, slabs, up_1, down_1, kappa, source, scratch, out):
    state, other, kappa_wide = scratch[:3]
    weights = scratch[3:7]
    rows = kappa.shape[0]
    for field in (other, kappa_wide):
        clear_edges(field)
    fill(
        kappa_wide,
        [
            (up_1, STEPS, STEPS, 0),
            (kappa, 0, rows, STEPS),
            (down_1, STEPS, STEPS, STEPS + rows),
        ],
    )
    face_weights(kappa_wide, weights, ALONG_THIRD)

    def heat(row, end):
        if row < STEPS:
            return up_1[2 * STEPS + row - 1 : 2 * STEPS + end - 1]
        if row < STEPS + rows:
            return source[row - STEPS : end - STEPS]
        return down_1[STEPS + row - rows : STEPS + end - rows]

    inside = inside_of(where[1], slabs, STEPS, rows)
    src, dst = state, other
    for step in range(1, STEPS + 1):
        count = rows + 2 * (STEPS - step)
        sweep(
            src, dst, weights, heat, step, count, 0, inside, out if step == STEPS else None
        )
        src, dst = dst, src


def phase_one_kernel(
    slabs, where, up_1, down_1, guess, initial, kappa, source, kappa_c,
    state_out, first_out, last_out, *scratch,
):
    state = scratch[0]
    rows = kappa.shape[0]
    clear_edges(state)
    fill(state, [(up_1, 0, STEPS, 0), (down_1, 0, STEPS, STEPS + rows)])

    @pl.when(where[0] == 15)
    def _():
        fill(state, [(initial, 0, rows, STEPS)])

    @pl.when(where[0] != 15)
    def _():
        fill(state, [(guess, 0, rows, STEPS)])

    def out(rows, value):
        state_out[rows] = value

    four_steps(where, slabs, up_1, down_1, kappa, source, scratch, out)

    @pl.when(where[0] == 14)
    def _():
        state_out[...] = initial[...]

    first_out[:STEPS] = state_out[:STEPS]
    last_out[:STEPS] = state_out[rows - STEPS :]
    half = kappa_c.shape[1]
    for row in range(rows // 2):
        at = (STEPS + row // 2, slice(row % 2 * half, (row % 2 + 1) * half))
        first_out[at] = kappa_c[row]
        last_out[at] = kappa_c[row]


def phase_two_kernel(
    slabs, where, up_1, down_1, up_2, down_2, before, initial, kappa, source,
    second_out, first_out, last_out, *scratch,
):
    state = scratch[0]
    rows = kappa.shape[0]
    clear_edges(state)
    fill(
        state,
        [
            (up_2, 0, STEPS, 0),
            (before, 0, rows, STEPS),
            (down_2, 0, STEPS, STEPS + rows),
        ],
    )

    def out(rows, value):
        second_out[rows] = value

    four_steps(where, slabs, up_1, down_1, kappa, source, scratch, out)

    @pl.when(where[0] == 13)
    def _():
        first_out[:STEPS] = initial[:STEPS]
        last_out[:STEPS] = initial[rows - STEPS :]

    @pl.when(where[0] != 13)
    def _():
        first_out[:STEPS] = second_out[:STEPS]
        last_out[:STEPS] = second_out[rows - STEPS :]

    first_out[STEPS:] = down_2[STEPS:]
    last_out[STEPS:] = up_2[STEPS:]


def coarse_kappa_4(field, up_2, down_2, kappa_c, at):
    block, half = kappa_c.shape[:2]
    clear_edges(field)
    fill(field, [(kappa_c, 0, block, at + block)])
    for row in range(block):
        piece = (STEPS + row // 2, slice(row % 2 * half, (row % 2 + 1) * half))
        field[at + row, PAD : PAD + half] = up_2[piece]
        field[at + 2 * block + row, PAD : PAD + half] = down_2[piece]


def coarse_scratch(rows, width, depth, fields):
    padded = pltpu.VMEM((rows, width + 2 * PAD, depth), jnp.float32)
    plain = pltpu.VMEM((rows, width, depth), jnp.float32)
    return [padded] * fields + [padded, plain, padded, plain, plain]


def phase_three_kernel(
    slabs, where, up_1, down_1, up_2, down_2, up_3, down_3, second, initial, kappa,
    source, kappa_c, _, third_out, tau_out, *scratch,
):
    state, other = scratch[:2]
    base, spare, kappa_wide, *weights = scratch[7:14]
    pair = scratch[14]
    rows, width = kappa.shape[:2]
    block, half = kappa_c.shape[:2]
    clear_edges(state)
    fill(state, [(up_3, 0, STEPS, 0), (down_3, 0, STEPS, STEPS + rows)])

    @pl.when(where[0] == 13)
    def _():
        fill(state, [(initial, 0, rows, STEPS)])

    @pl.when(where[0] != 13)
    def _():
        fill(state, [(second, 0, rows, STEPS)])

    clear_edges(base)
    for row in range(block + 2):
        fine_row = STEPS - 2 + 2 * row
        pair[...] = (
            state[fine_row, PAD : PAD + width] + state[fine_row + 1, PAD : PAD + width]
        )
        base[row, PAD : PAD + half] = 0.25 * (
            pair[pl.ds(0, half, stride=2), :] + pair[pl.ds(1, half, stride=2), :]
        )

    def out(rows, value):
        third_out[rows] = value

    four_steps(where, slabs, up_1, down_1, kappa, source, scratch, out)

    coarse_kappa_4(kappa_wide, up_2, down_2, kappa_c, 0)
    face_weights(kappa_wide, weights, 4.0 * ALONG_THIRD)

    def keep(rows, value):
        tau_out[rows] = value

    sweep(base, spare, weights, None, 1, block, block - 1, lambda row: (0, None), keep)
    use = jnp.where(where[0] == 13, 0.0, 1.0)
    for row in range(block):
        pair[...] = third_out[2 * row] + third_out[2 * row + 1]
        now = 0.25 * (
            pair[pl.ds(0, half, stride=2), :] + pair[pl.ds(1, half, stride=2), :]
        )
        tau_out[row] = now - use * tau_out[row]


def near_sums_kernel(
    slabs, where, got_3, got_2, got_1, tau, up_2, down_2, kappa_c, both_out, *scratch
):
    ahead, wrapped, spare, kappa_wide, *weights = scratch
    block, half = kappa_c.shape[:2]
    local = lax.rem(where[0], GROUP)
    high = where[0] >= GROUP
    for field in (ahead, wrapped, spare):
        clear_edges(field)
    coarse_kappa_4(kappa_wide, up_2, down_2, kappa_c, 0)
    face_weights(kappa_wide, weights, 4.0 * ALONG_THIRD)
    inside = inside_of(where[1], slabs, block, block)
    for is_ahead in (True, False):
        src, dst = (ahead, spare) if is_ahead else (wrapped, spare)
        for distance, got in ((3, got_3), (2, got_2), (1, got_1)):
            apart = high & (local >= 5) & (local < distance + 5)
            use = (local >= distance) & ~apart if is_ahead else local < distance
            use = jnp.where(use, 1.0, 0.0)
            for row in range(block + 2 * distance):
                at = (row + block - distance, slice(PAD, PAD + half))
                value = use * got[row]
                src[at] = value if distance == 3 else src[at] + value
            if distance == 1:

                def out(rows, value, is_ahead=is_ahead):
                    if is_ahead:
                        both_out[0, rows] = value + tau[rows]
                    else:
                        both_out[1, rows] = value

            else:
                out = None
            sweep(
                src, dst, weights, None, block - distance + 1, block + 2 * distance - 2,
                0, inside, out,
            )
            src, dst = dst, src


def far_sums_kernel(
    slabs, where, got_up, got, got_down, both, up_2, down_2, kappa_c,
    ahead_out, wrapped_out, last_out, *scratch,
):
    field, spare, kappa_wide, *weights = scratch
    block, half = kappa_c.shape[:2]
    local = lax.rem(where[0], GROUP)
    high = where[0] >= GROUP
    clear_edges(field)
    clear_edges(spare)
    coarse_kappa_4(kappa_wide, up_2, down_2, kappa_c, 0)
    face_weights(kappa_wide, weights, 4.0 * ALONG_THIRD)
    inside = inside_of(where[1], slabs, block, block)
    late = local >= 4
    to_ahead = jnp.where(late & ~(high & (local >= 5)), 1.0, 0.0)
    from_wrapped = jnp.where(late, 1.0, 0.0)
    from_ahead = jnp.where(late | (high & (local == 0)), 0.0, 1.0)
    for index, result in ((0, ahead_out), (1, wrapped_out)):
        for piece, ref in enumerate((got_up, got, got_down)):
            for row in range(block):
                at = (piece * block + row, slice(PAD, PAD + half))
                if index == 0:
                    field[at] = to_ahead * ref[0, row]
                else:
                    field[at] = from_wrapped * ref[1, row] + from_ahead * ref[0, row]

        def out(rows, value, index=index, result=result):
            result[rows] = value + both[index, rows]

        src, dst = field, spare
        for step in range(1, block + 1):
            count = 3 * block - 2 * step
            sweep(
                src, dst, weights, None, step, count, 0, inside,
                out if step == block else None,
            )
            src, dst = dst, src
    hand_wrapped = high & (local < 5)

    @pl.when(hand_wrapped)
    def _():
        last_out[...] = wrapped_out[...]

    @pl.when(jnp.logical_not(hand_wrapped))
    def _():
        last_out[...] = ahead_out[...]


def hand_over_kernel(
    slabs, where, far_up, near_up, last, near_down, far_down, up_2, down_2, up_3, down_3,
    kappa_c, ahead, wrapped, handed_out, kept_out, *scratch,
):
    field, spare, kappa_wide, *weights = scratch
    block, half = kappa_c.shape[:2]
    local = lax.rem(where[0], GROUP)
    high = where[0] >= GROUP
    clear_edges(field)
    clear_edges(spare)
    coarse_kappa_4(kappa_wide, up_2, down_2, kappa_c, block)
    for row in range(block):
        piece = (STEPS + row // 2, slice(row % 2 * half, (row % 2 + 1) * half))
        kappa_wide[row, PAD : PAD + half] = up_3[piece]
        kappa_wide[4 * block + row, PAD : PAD + half] = down_3[piece]
    fill(
        field,
        [
            (far_up, 0, block, 0),
            (near_up, 0, block, block),
            (last, 0, block, 2 * block),
            (near_down, 0, block, 3 * block),
            (far_down, 0, block, 4 * block),
        ],
    )
    face_weights(kappa_wide, weights, 4.0 * ALONG_THIRD)
    inside = inside_of(where[1], slabs, 2 * block, block)
    early = local < 5

    def one(use):
        return jnp.where(use, 1.0, 0.0)

    hand_image = one(early & ~high)
    hand_wrapped = one(early)
    hand_ahead = one(~early)
    keep_image = one(high)
    keep_wrapped = one(high & ~early)
    keep_ahead = one(early)

    def out(rows, value):
        a, w = ahead[rows], wrapped[rows]
        handed_out[rows] = hand_image * value + hand_wrapped * w + hand_ahead * a
        kept_out[rows] = keep_image * value + keep_wrapped * w + keep_ahead * a

    src, dst = field, spare
    for step in range(1, 2 * block + 1):
        count = 5 * block - 2 * step
        sweep(
            src, dst, weights, None, step, count, 0, inside,
            out if step == 2 * block else None,
        )
        src, dst = dst, src


def call(kernel, slabs, outs, scratch, where, *args, unread=0):
    vmem = pl.BlockSpec(memory_space=pltpu.VMEM)
    anywhere = pl.BlockSpec(memory_space=pl.ANY)
    return pl.pallas_call(
        functools.partial(kernel, slabs),
        out_shape=[jax.ShapeDtypeStruct(shape, jnp.float32) for shape in outs],
        in_specs=[pl.BlockSpec(memory_space=pltpu.SMEM)]
        + [vmem] * (len(args) - unread)
        + [anywhere] * unread,
        out_specs=[vmem] * len(outs),
        scratch_shapes=scratch,
        compiler_params=pltpu.CompilerParams(vmem_limit_bytes=40 * 2**20),
        cost_estimate=pl.CostEstimate(flops=0, bytes_accessed=0, transcendentals=0),
    )(where, *args)


def per_device(initial, guess, conductivity, source):
    rows, width_two, width_three = conductivity.shape
    crows, half = rows // 2, width_two // 2
    slabs = lax.axis_size("space")
    tm = lax.axis_index("tm")
    sp = lax.axis_index("space")
    local = tm % GROUP
    where = jnp.stack([tm, sp]).astype(jnp.int32)

    def cut(array, have, want):
        return array[have - want : array.shape[0] - (have - want)]

    def route(block, pairs):
        return lax.ppermute(block, ("tm", "space"), pairs)

    def along_space(block, distance):
        pairs = [
            (i, i + distance) for i in range(slabs) if 0 <= i + distance < slabs
        ]
        return lax.ppermute(block, "space", pairs)

    def along_time(block, pairs):
        return lax.ppermute(block, "tm", pairs)

    def ring(shift):
        return [
            (g * GROUP + i, g * GROUP + (i + shift) % GROUP)
            for g in (0, 1)
            for i in range(GROUP)
        ]

    def restrict(field):
        return field.reshape(-1, 2, half, 2, width_three).mean(axis=(1, 3))

    def neighbours(block_first, block_last):
        return along_space(block_last, 1), along_space(block_first, -1)

    block_shape = (rows, width_two, width_three)
    coarse_shape = (crows, half, width_three)
    packed_shape = (STEPS + crows // 2, width_two, width_three)
    scratch = fine_scratch(rows, width_two, width_three)

    kappa_c = restrict(conductivity)
    ends = [
        jnp.where(tm == 15, initial[part], guess[0][part])
        for part in (slice(0, STEPS), slice(rows - STEPS, rows))
    ]
    sides = neighbours(
        jnp.concatenate([ends[0], conductivity[:STEPS], source[: STEPS - 1]]),
        jnp.concatenate([ends[1], conductivity[-STEPS:], source[1 - STEPS :]]),
    )
    state, first, last = call(
        phase_one_kernel, slabs, [block_shape, packed_shape, packed_shape], scratch,
        where, *sides, guess[0], initial, conductivity, source, kappa_c,
    )
    sides_2 = neighbours(first, last)
    second, first, last = call(
        phase_two_kernel, slabs, [block_shape, packed_shape, packed_shape], scratch,
        where, *sides, *sides_2, state, initial, conductivity, source,
    )
    sides_3 = neighbours(first, last)
    second_near = along_time(second, ring(2))
    second_far = along_time(second_near, [(0, 8), (1, 9), (8, 0), (9, 1)])
    third, tau = call(
        phase_three_kernel, slabs, [block_shape, coarse_shape],
        scratch
        + coarse_scratch(3 * crows, half, width_three, 2)
        + [pltpu.VMEM((width_two, width_three), jnp.float32)],
        where, *sides, *sides_2, *sides_3, second, initial, conductivity, source, kappa_c,
        second_near, unread=1,
    )

    up, down = neighbours(tau, tau)
    tau_wide = jnp.concatenate([up, tau, down], 0)
    got = [along_time(cut(tau_wide, crows, d), ring(d)) for d in (3, 2, 1)]
    third_far = along_time(
        third, [(i, (i + 3) % (2 * GROUP)) for i in (5, 6, 7, 13, 14, 15)]
    )
    (both,) = call(
        near_sums_kernel, slabs, [(2,) + coarse_shape],
        coarse_scratch(3 * crows, half, width_three, 3),
        where, *got, tau, *sides_2, kappa_c,
    )

    def diagonal(distance):
        pairs = [
            (t * slabs + i, u * slabs + i + distance)
            for t, u in ring(4)
            for i in range(slabs)
            if 0 <= i + distance < slabs
        ]
        return route(both, pairs)

    got = [diagonal(1), diagonal(0), diagonal(-1)]
    ahead, wrapped, last = call(
        far_sums_kernel, slabs, [coarse_shape] * 3,
        coarse_scratch(3 * crows, half, width_three, 2),
        where, *got, both, *sides_2, kappa_c,
    )

    third_near = along_time(lax.optimization_barrier((third, last))[0], ring(3))
    near = neighbours(last, last)
    far = (along_space(last, 2), along_space(last, -2))
    handed, kept = call(
        hand_over_kernel, slabs, [coarse_shape] * 2,
        coarse_scratch(5 * crows, half, width_three, 2),
        where, far[0], near[0], last, near[1], far[1], *sides_2, *sides_3, kappa_c,
        ahead, wrapped,
    )
    handed = along_time(
        handed,
        [
            (g * GROUP + i, (1 - g) * GROUP + (i + 3) % GROUP)
            for g in (0, 1)
            for i in range(GROUP)
        ],
    )
    kept = along_time(kept, ring(3))
    second_far, third_far = lax.optimization_barrier((second_far, third_far, kept))[:2]
    third_home = jnp.where(local < 3, third_far, third_near)
    second_home = jnp.where(local < 2, second_far, second_near)

    residual = third_home - second_home
    change = handed + kept - restrict(second_home)
    finer = jnp.repeat(jnp.repeat(change, 2, axis=0), 2, axis=1)
    corrected = second_home + finer
    return (corrected[None], residual[None])


def solution(mesh):
    in_specs = (
        P("space", None, None),
        P("tm", "space", None, None),
        P("space", None, None),
        P("space", None, None),
    )
    out_specs = (P("tm", "space", None, None), P("tm", "space", None, None))
    return jax.shard_map(
        per_device, mesh=mesh, in_specs=in_specs, out_specs=out_specs, check_vma=False
    )
```

```python
import functools

import jax
import jax.numpy as jnp
from jax import lax
from jax.experimental import pallas as pl
from jax.experimental.pallas import tpu as pltpu
from jax.sharding import PartitionSpec as P

STEPS = 4
ALONG_FIRST = 0.1
ALONG_SECOND = 0.1
ALONG_THIRD = 0.0125
GROUP = 8
PAD = 8


def lane_mask(shape, *lanes):
    lane = lax.broadcasted_iota(jnp.int32, shape, 1)
    hit = lane == lanes[0]
    for other in lanes[1:]:
        hit = hit | (lane == other)
    return hit


def clear_edges(field):
    rows, wide, depth = field.shape
    zero = jnp.zeros((rows, PAD, depth), jnp.float32)
    field[:, :PAD] = zero
    field[:, wide - PAD :] = zero


def face_weights(kappa, weights, third):
    by_first, by_second, by_third, keep = weights
    rows, wide, depth = kappa.shape
    width = wide - 2 * PAD
    first_w, third_w = 0.5 * ALONG_FIRST, 0.5 * third
    inner = slice(PAD, PAD + width)
    for row in range(rows):
        k = kappa[row, inner]
        if row:
            by_first[row] = first_w * (kappa[row - 1, inner] + k)
        by_second[row, inner] = first_w * (kappa[row, PAD - 1 : PAD - 1 + width] + k)
        by_second[row, PAD + width :] = (
            first_w * kappa[row, PAD + width - 1 : 2 * PAD + width - 1]
        )
        deeper = pltpu.roll(k, depth - 1, 1)
        by_third[row] = jnp.where(
            lane_mask(k.shape, depth - 1), 0.0, third_w * (k + deeper)
        )
        keep[row] = jnp.where(lane_mask(k.shape, 0, depth - 1), 1.0 - third_w * k, 1.0)


def sweep(src, dst, weights, heat, first, count, shift, inside, out=None):
    by_first, by_second, by_third, keep = weights
    wide, depth = src.shape[1:]
    width = wide - 2 * PAD
    most = max(1, 256 // width)
    inner = slice(PAD, PAD + width)
    upper = slice(PAD + 1, PAD + 1 + width)
    lower = slice(PAD - 1, PAD - 1 + width)
    row = first
    while row < first + count:
        key, mask = inside(row)
        end = row + 1
        while end < first + count and end - row < most and inside(end)[0] == key:
            end += 1
        here = slice(row, end)
        w = slice(row + shift, end + shift)
        v = src[here, inner]
        total = by_first[row + shift + 1 : end + shift + 1] * (
            src[row + 1 : end + 1, inner] - v
        ) - by_first[w] * (v - src[row - 1 : end - 1, inner])
        total = total + (
            by_second[w, upper] * (src[here, upper] - v)
            - by_second[w, inner] * (v - src[here, lower])
        )
        deep = by_third[w] * (pltpu.roll(v, depth - 1, 2) - v)
        total = keep[w] * v + (total + (deep - pltpu.roll(deep, 1, 2)))
        if heat is not None:
            total = total + heat(row, end)
        if mask is not None:
            total = total * mask
        if out is None:
            dst[here, inner] = total
        else:
            out(slice(row - first, end - first), total)
        row = end


def inside_of(place, slabs, margin, block):
    def inside(row):
        if row < margin:
            need = (margin - row + block - 1) // block
            return -need, jnp.where(place >= need, 1.0, 0.0)
        if row >= margin + block:
            need = (row - margin) // block
            return need, jnp.where(place + need < slabs, 1.0, 0.0)
        return 0, None

    return inside


def fill(field, pieces):
    width = field.shape[1] - 2 * PAD
    for ref, first, count, row in pieces:
        field[row : row + count, PAD : PAD + width] = ref[first : first + count]


def fine_scratch(rows, width, depth):
    high = rows + 2 * STEPS
    padded = pltpu.VMEM((high, width + 2 * PAD, depth), jnp.float32)
    plain = pltpu.VMEM((high, width, depth), jnp.float32)
    return [padded, padded, padded, plain, padded, plain, plain]


def four_steps(where, slabs, up_1, down_1, kappa, source, scratch, out):
    state, other, kappa_wide = scratch[:3]
    weights = scratch[3:7]
    rows = kappa.shape[0]
    for field in (other, kappa_wide):
        clear_edges(field)
    fill(
        kappa_wide,
        [
            (up_1, STEPS, STEPS, 0),
            (kappa, 0, rows, STEPS),
            (down_1, STEPS, STEPS, STEPS + rows),
        ],
    )
    face_weights(kappa_wide, weights, ALONG_THIRD)

    def heat(row, end):
        if row < STEPS:
            return up_1[2 * STEPS + row - 1 : 2 * STEPS + end - 1]
        if row < STEPS + rows:
            return source[row - STEPS : end - STEPS]
        return down_1[STEPS + row - rows : STEPS + end - rows]

    inside = inside_of(where[1], slabs, STEPS, rows)
    src, dst = state, other
    for step in range(1, STEPS + 1):
        count = rows + 2 * (STEPS - step)
        sweep(
            src, dst, weights, heat, step, count, 0, inside, out if step == STEPS else None
        )
        src, dst = dst, src


def first_ends_kernel(where, guess, initial, kappa, source, first_out, last_out):
    rows = kappa.shape[0]
    start = where[0] == 15
    for out, at, heat in ((first_out, 0, 0), (last_out, rows - STEPS, rows - STEPS + 1)):

        @pl.when(start)
        def _(out=out, at=at):
            out[:STEPS] = initial[at : at + STEPS]

        @pl.when(jnp.logical_not(start))
        def _(out=out, at=at):
            out[:STEPS] = guess[at : at + STEPS]

        out[STEPS : 2 * STEPS] = kappa[at : at + STEPS]
        out[2 * STEPS :] = source[heat : heat + STEPS - 1]


def phase_one_kernel(
    slabs, where, up_1, down_1, guess, initial, kappa, source, kappa_c,
    state_out, first_out, last_out, *scratch,
):
    state = scratch[0]
    rows = kappa.shape[0]
    clear_edges(state)
    fill(state, [(up_1, 0, STEPS, 0), (down_1, 0, STEPS, STEPS + rows)])

    @pl.when(where[0] == 15)
    def _():
        fill(state, [(initial, 0, rows, STEPS)])

    @pl.when(where[0] != 15)
    def _():
        fill(state, [(guess, 0, rows, STEPS)])

    def out(rows, value):
        state_out[rows] = value

    four_steps(where, slabs, up_1, down_1, kappa, source, scratch, out)

    @pl.when(where[0] == 14)
    def _():
        state_out[...] = initial[...]

    first_out[:STEPS] = state_out[:STEPS]
    last_out[:STEPS] = state_out[rows - STEPS :]
    half = kappa_c.shape[1]
    for row in range(rows // 2):
        at = (STEPS + row // 2, slice(row % 2 * half, (row % 2 + 1) * half))
        first_out[at] = kappa_c[row]
        last_out[at] = kappa_c[row]


def phase_two_kernel(
    slabs, where, up_1, down_1, up_2, down_2, before, initial, kappa, source,
    second_out, first_out, last_out, *scratch,
):
    state = scratch[0]
    rows = kappa.shape[0]
    clear_edges(state)
    fill(
        state,
        [
            (up_2, 0, STEPS, 0),
            (before, 0, rows, STEPS),
            (down_2, 0, STEPS, STEPS + rows),
        ],
    )

    def out(rows, value):
        second_out[rows] = value

    four_steps(where, slabs, up_1, down_1, kappa, source, scratch, out)

    @pl.when(where[0] == 13)
    def _():
        first_out[:STEPS] = initial[:STEPS]
        last_out[:STEPS] = initial[rows - STEPS :]

    @pl.when(where[0] != 13)
    def _():
        first_out[:STEPS] = second_out[:STEPS]
        last_out[:STEPS] = second_out[rows - STEPS :]

    first_out[STEPS:] = down_2[STEPS:]
    last_out[STEPS:] = up_2[STEPS:]


def coarse_kappa_4(field, up_2, down_2, kappa_c, at):
    block, half = kappa_c.shape[:2]
    clear_edges(field)
    fill(field, [(kappa_c, 0, block, at + block)])
    for row in range(block):
        piece = (STEPS + row // 2, slice(row % 2 * half, (row % 2 + 1) * half))
        field[at + row, PAD : PAD + half] = up_2[piece]
        field[at + 2 * block + row, PAD : PAD + half] = down_2[piece]


def coarse_scratch(rows, width, depth, fields):
    padded = pltpu.VMEM((rows, width + 2 * PAD, depth), jnp.float32)
    plain = pltpu.VMEM((rows, width, depth), jnp.float32)
    return [padded] * fields + [padded, plain, padded, plain, plain]


def phase_three_kernel(
    slabs, where, up_1, down_1, up_2, down_2, up_3, down_3, second, initial, kappa,
    source, kappa_c, second_near, third_out, tau_out, cross_out, *scratch,
):
    state, other = scratch[:2]
    base, spare, kappa_wide, *weights = scratch[7:14]
    pair = scratch[14]
    rows, width = kappa.shape[:2]
    block, half = kappa_c.shape[:2]
    clear_edges(state)
    fill(state, [(up_3, 0, STEPS, 0), (down_3, 0, STEPS, STEPS + rows)])

    @pl.when(where[0] == 13)
    def _():
        fill(state, [(initial, 0, rows, STEPS)])

    @pl.when(where[0] != 13)
    def _():
        fill(state, [(second, 0, rows, STEPS)])

    clear_edges(base)
    for row in range(block + 2):
        fine_row = STEPS - 2 + 2 * row
        pair[...] = (
            state[fine_row, PAD : PAD + width] + state[fine_row + 1, PAD : PAD + width]
        )
        base[row, PAD : PAD + half] = 0.25 * (
            pair[pl.ds(0, half, stride=2), :] + pair[pl.ds(1, half, stride=2), :]
        )

    def out(rows, value):
        third_out[rows] = value

    four_steps(where, slabs, up_1, down_1, kappa, source, scratch, out)

    @pl.when(lax.rem(where[0], GROUP) < 2)
    def _():
        cross_out[...] = second_near[...]

    @pl.when(lax.rem(where[0], GROUP) >= 2)
    def _():
        cross_out[...] = third_out[...]

    coarse_kappa_4(kappa_wide, up_2, down_2, kappa_c, 0)
    face_weights(kappa_wide, weights, 4.0 * ALONG_THIRD)

    def keep(rows, value):
        tau_out[rows] = value

    sweep(base, spare, weights, None, 1, block, block - 1, lambda row: (0, None), keep)
    use = jnp.where(where[0] == 13, 0.0, 1.0)
    for row in range(block):
        pair[...] = third_out[2 * row] + third_out[2 * row + 1]
        now = 0.25 * (
            pair[pl.ds(0, half, stride=2), :] + pair[pl.ds(1, half, stride=2), :]
        )
        tau_out[row] = now - use * tau_out[row]


def near_sums_kernel(
    slabs, where, got_3, got_2, got_1, tau, up_2, down_2, kappa_c, both_out, *scratch
):
    ahead, wrapped, spare, kappa_wide, *weights = scratch
    block, half = kappa_c.shape[:2]
    local = lax.rem(where[0], GROUP)
    high = where[0] >= GROUP
    for field in (ahead, wrapped, spare):
        clear_edges(field)
    coarse_kappa_4(kappa_wide, up_2, down_2, kappa_c, 0)
    face_weights(kappa_wide, weights, 4.0 * ALONG_THIRD)
    inside = inside_of(where[1], slabs, block, block)
    for is_ahead in (True, False):
        src, dst = (ahead, spare) if is_ahead else (wrapped, spare)
        for distance, got in ((3, got_3), (2, got_2), (1, got_1)):
            apart = high & (local >= 5) & (local < distance + 5)
            use = (local >= distance) & ~apart if is_ahead else local < distance
            use = jnp.where(use, 1.0, 0.0)
            for row in range(block + 2 * distance):
                at = (row + block - distance, slice(PAD, PAD + half))
                value = use * got[row]
                src[at] = value if distance == 3 else src[at] + value
            if distance == 1:

                def out(rows, value, is_ahead=is_ahead):
                    if is_ahead:
                        both_out[0, rows] = value + tau[rows]
                    else:
                        both_out[1, rows] = value

            else:
                out = None
            sweep(
                src, dst, weights, None, block - distance + 1, block + 2 * distance - 2,
                0, inside, out,
            )
            src, dst = dst, src


def far_sums_kernel(
    slabs, where, got_up, got, got_down, both, up_2, down_2, kappa_c, _,
    ahead_out, wrapped_out, last_out, *scratch,
):
    field, spare, kappa_wide, *weights = scratch
    block, half = kappa_c.shape[:2]
    local = lax.rem(where[0], GROUP)
    high = where[0] >= GROUP
    clear_edges(field)
    clear_edges(spare)
    coarse_kappa_4(kappa_wide, up_2, down_2, kappa_c, 0)
    face_weights(kappa_wide, weights, 4.0 * ALONG_THIRD)
    inside = inside_of(where[1], slabs, block, block)
    late = local >= 4
    to_ahead = jnp.where(late & ~(high & (local >= 5)), 1.0, 0.0)
    from_wrapped = jnp.where(late, 1.0, 0.0)
    from_ahead = jnp.where(late | (high & (local == 0)), 0.0, 1.0)
    for index, result in ((0, ahead_out), (1, wrapped_out)):
        for piece, ref in enumerate((got_up, got, got_down)):
            for row in range(block):
                at = (piece * block + row, slice(PAD, PAD + half))
                if index == 0:
                    field[at] = to_ahead * ref[0, row]
                else:
                    field[at] = from_wrapped * ref[1, row] + from_ahead * ref[0, row]

        def out(rows, value, index=index, result=result):
            result[rows] = value + both[index, rows]

        src, dst = field, spare
        for step in range(1, block + 1):
            count = 3 * block - 2 * step
            sweep(
                src, dst, weights, None, step, count, 0, inside,
                out if step == block else None,
            )
            src, dst = dst, src
    hand_wrapped = high & (local < 5)

    @pl.when(hand_wrapped)
    def _():
        last_out[...] = wrapped_out[...]

    @pl.when(jnp.logical_not(hand_wrapped))
    def _():
        last_out[...] = ahead_out[...]


def hand_over_kernel(
    slabs, where, far_up, near_up, last, near_down, far_down, up_2, down_2, up_3, down_3,
    kappa_c, ahead, wrapped, handed_out, kept_out, *scratch,
):
    field, spare, kappa_wide, *weights = scratch
    block, half = kappa_c.shape[:2]
    local = lax.rem(where[0], GROUP)
    high = where[0] >= GROUP
    clear_edges(field)
    clear_edges(spare)
    coarse_kappa_4(kappa_wide, up_2, down_2, kappa_c, block)
    for row in range(block):
        piece = (STEPS + row // 2, slice(row % 2 * half, (row % 2 + 1) * half))
        kappa_wide[row, PAD : PAD + half] = up_3[piece]
        kappa_wide[4 * block + row, PAD : PAD + half] = down_3[piece]
    fill(
        field,
        [
            (far_up, 0, block, 0),
            (near_up, 0, block, block),
            (last, 0, block, 2 * block),
            (near_down, 0, block, 3 * block),
            (far_down, 0, block, 4 * block),
        ],
    )
    face_weights(kappa_wide, weights, 4.0 * ALONG_THIRD)
    inside = inside_of(where[1], slabs, 2 * block, block)
    early = local < 5

    def one(use):
        return jnp.where(use, 1.0, 0.0)

    hand_image = one(early & ~high)
    hand_wrapped = one(early)
    hand_ahead = one(~early)
    keep_image = one(high)
    keep_wrapped = one(high & ~early)
    keep_ahead = one(early)

    def out(rows, value):
        a, w = ahead[rows], wrapped[rows]
        handed_out[rows] = hand_image * value + hand_wrapped * w + hand_ahead * a
        kept_out[rows] = keep_image * value + keep_wrapped * w + keep_ahead * a

    src, dst = field, spare
    for step in range(1, 2 * block + 1):
        count = 5 * block - 2 * step
        sweep(
            src, dst, weights, None, step, count, 0, inside,
            out if step == 2 * block else None,
        )
        src, dst = dst, src


def call(kernel, slabs, outs, scratch, where, *args, unread=0):
    vmem = pl.BlockSpec(memory_space=pltpu.VMEM)
    anywhere = pl.BlockSpec(memory_space=pl.ANY)
    return pl.pallas_call(
        kernel if slabs is None else functools.partial(kernel, slabs),
        out_shape=[jax.ShapeDtypeStruct(shape, jnp.float32) for shape in outs],
        in_specs=[pl.BlockSpec(memory_space=pltpu.SMEM)]
        + [vmem] * (len(args) - unread)
        + [anywhere] * unread,
        out_specs=[vmem] * len(outs),
        scratch_shapes=scratch,
        compiler_params=pltpu.CompilerParams(vmem_limit_bytes=40 * 2**20),
        cost_estimate=pl.CostEstimate(flops=0, bytes_accessed=0, transcendentals=0),
    )(where, *args)


def per_device(initial, guess, conductivity, source):
    rows, width_two, width_three = conductivity.shape
    crows, half = rows // 2, width_two // 2
    slabs = lax.axis_size("space")
    tm = lax.axis_index("tm")
    sp = lax.axis_index("space")
    local = tm % GROUP
    where = jnp.stack([tm, sp]).astype(jnp.int32)

    def cut(array, have, want):
        return array[have - want : array.shape[0] - (have - want)]

    def route(block, pairs):
        return lax.ppermute(block, ("tm", "space"), pairs)

    def along_space(block, distance):
        pairs = [
            (i, i + distance) for i in range(slabs) if 0 <= i + distance < slabs
        ]
        return lax.ppermute(block, "space", pairs)

    def along_time(block, pairs):
        return lax.ppermute(block, "tm", pairs)

    def ring(shift):
        return [
            (g * GROUP + i, g * GROUP + (i + shift) % GROUP)
            for g in (0, 1)
            for i in range(GROUP)
        ]

    def restrict(field):
        return field.reshape(-1, 2, half, 2, width_three).mean(axis=(1, 3))

    def neighbours(block_first, block_last):
        return along_space(block_last, 1), along_space(block_first, -1)

    block_shape = (rows, width_two, width_three)
    coarse_shape = (crows, half, width_three)
    packed_shape = (STEPS + crows // 2, width_two, width_three)
    scratch = fine_scratch(rows, width_two, width_three)

    kappa_c = restrict(conductivity)
    first, last = call(
        first_ends_kernel, None, [(3 * STEPS - 1, width_two, width_three)] * 2, [],
        where, guess[0], initial, conductivity, source,
    )
    sides = neighbours(first, last)
    state, first, last = call(
        phase_one_kernel, slabs, [block_shape, packed_shape, packed_shape], scratch,
        where, *sides, guess[0], initial, conductivity, source, kappa_c,
    )
    sides_2 = neighbours(first, last)
    second, first, last = call(
        phase_two_kernel, slabs, [block_shape, packed_shape, packed_shape], scratch,
        where, *sides, *sides_2, state, initial, conductivity, source,
    )
    sides_3 = neighbours(first, last)
    second_near = along_time(second, ring(2))
    third, tau, crossed = call(
        phase_three_kernel, slabs, [block_shape, coarse_shape, block_shape],
        scratch
        + coarse_scratch(3 * crows, half, width_three, 2)
        + [pltpu.VMEM((width_two, width_three), jnp.float32)],
        where, *sides, *sides_2, *sides_3, second, initial, conductivity, source, kappa_c,
        second_near,
    )

    up, down = neighbours(tau, tau)
    tau_wide = jnp.concatenate([up, tau, down], 0)
    got = [along_time(cut(tau_wide, crows, d), ring(d)) for d in (3, 2, 1)]
    crossed = along_time(
        crossed,
        [(i, i ^ GROUP) for i in range(2 * GROUP) if i % GROUP in (0, 1, 5, 6, 7)],
    )
    (both,) = call(
        near_sums_kernel, slabs, [(2,) + coarse_shape],
        coarse_scratch(3 * crows, half, width_three, 3),
        where, *got, tau, *sides_2, kappa_c,
    )

    def diagonal(distance):
        pairs = [
            (t * slabs + i, u * slabs + i + distance)
            for t, u in ring(4)
            for i in range(slabs)
            if 0 <= i + distance < slabs
        ]
        return route(both, pairs)

    got = [diagonal(1), diagonal(0), diagonal(-1)]
    ahead, wrapped, last = call(
        far_sums_kernel, slabs, [coarse_shape] * 3,
        coarse_scratch(3 * crows, half, width_three, 2),
        where, *got, both, *sides_2, kappa_c, crossed, unread=1,
    )

    third_home = along_time(
        lax.optimization_barrier((jnp.where(local >= 5, crossed, third), last))[0],
        ring(3),
    )
    near = neighbours(last, last)
    far = (along_space(last, 2), along_space(last, -2))
    handed, kept = call(
        hand_over_kernel, slabs, [coarse_shape] * 2,
        coarse_scratch(5 * crows, half, width_three, 2),
        where, far[0], near[0], last, near[1], far[1], *sides_2, *sides_3, kappa_c,
        ahead, wrapped,
    )
    handed = along_time(
        handed,
        [
            (g * GROUP + i, (1 - g) * GROUP + (i + 3) % GROUP)
            for g in (0, 1)
            for i in range(GROUP)
        ],
    )
    kept = along_time(kept, ring(3))
    second_home = jnp.where(local < 2, crossed, second_near)

    residual = third_home - second_home
    change = handed + kept - restrict(second_home)
    finer = jnp.repeat(jnp.repeat(change, 2, axis=0), 2, axis=1)
    corrected = second_home + finer
    return (corrected[None], residual[None])


def solution(mesh):
    in_specs = (
        P("space", None, None),
        P("tm", "space", None, None),
        P("space", None, None),
        P("space", None, None),
    )
    out_specs = (P("tm", "space", None, None), P("tm", "space", None, None))
    return jax.shard_map(
        per_device, mesh=mesh, in_specs=in_specs, out_specs=out_specs, check_vma=False
    )
```

```python
import functools

import jax
import jax.numpy as jnp
from jax import lax
from jax.experimental import pallas as pl
from jax.experimental.pallas import tpu as pltpu
from jax.sharding import PartitionSpec as P

STEPS = 4
ALONG_FIRST = 0.1
ALONG_SECOND = 0.1
ALONG_THIRD = 0.0125
GROUP = 8
PAD = 8


def lane_mask(shape, *lanes):
    lane = lax.broadcasted_iota(jnp.int32, shape, 1)
    hit = lane == lanes[0]
    for other in lanes[1:]:
        hit = hit | (lane == other)
    return hit


def clear_edges(field):
    rows, wide, depth = field.shape
    zero = jnp.zeros((rows, PAD, depth), jnp.float32)
    field[:, :PAD] = zero
    field[:, wide - PAD :] = zero


def face_weights(kappa, weights, third):
    by_first, by_second, by_third, keep = weights
    rows, wide, depth = kappa.shape
    width = wide - 2 * PAD
    first_w, third_w = 0.5 * ALONG_FIRST, 0.5 * third
    inner = slice(PAD, PAD + width)
    for row in range(rows):
        k = kappa[row, inner]
        if row:
            by_first[row] = first_w * (kappa[row - 1, inner] + k)
        by_second[row, inner] = first_w * (kappa[row, PAD - 1 : PAD - 1 + width] + k)
        by_second[row, PAD + width :] = (
            first_w * kappa[row, PAD + width - 1 : 2 * PAD + width - 1]
        )
        deeper = pltpu.roll(k, depth - 1, 1)
        by_third[row] = jnp.where(
            lane_mask(k.shape, depth - 1), 0.0, third_w * (k + deeper)
        )
        keep[row] = jnp.where(lane_mask(k.shape, 0, depth - 1), 1.0 - third_w * k, 1.0)


def sweep(src, dst, weights, heat, first, count, shift, inside, out=None):
    by_first, by_second, by_third, keep = weights
    wide, depth = src.shape[1:]
    width = wide - 2 * PAD
    most = max(1, 256 // width)
    inner = slice(PAD, PAD + width)
    upper = slice(PAD + 1, PAD + 1 + width)
    lower = slice(PAD - 1, PAD - 1 + width)
    row = first
    while row < first + count:
        key, mask = inside(row)
        end = row + 1
        while end < first + count and end - row < most and inside(end)[0] == key:
            end += 1
        here = slice(row, end)
        w = slice(row + shift, end + shift)
        v = src[here, inner]
        total = by_first[row + shift + 1 : end + shift + 1] * (
            src[row + 1 : end + 1, inner] - v
        ) - by_first[w] * (v - src[row - 1 : end - 1, inner])
        total = total + (
            by_second[w, upper] * (src[here, upper] - v)
            - by_second[w, inner] * (v - src[here, lower])
        )
        deep = by_third[w] * (pltpu.roll(v, depth - 1, 2) - v)
        total = keep[w] * v + (total + (deep - pltpu.roll(deep, 1, 2)))
        if heat is not None:
            total = total + heat(row, end)
        if mask is not None:
            total = total * mask
        if out is None:
            dst[here, inner] = total
        else:
            out(slice(row - first, end - first), total)
        row = end


def inside_of(place, slabs, margin, block):
    def inside(row):
        if row < margin:
            need = (margin - row + block - 1) // block
            return -need, jnp.where(place >= need, 1.0, 0.0)
        if row >= margin + block:
            need = (row - margin) // block
            return need, jnp.where(place + need < slabs, 1.0, 0.0)
        return 0, None

    return inside


def fill(field, pieces):
    width = field.shape[1] - 2 * PAD
    for ref, first, count, row in pieces:
        field[row : row + count, PAD : PAD + width] = ref[first : first + count]


def fine_scratch(rows, width, depth):
    high = rows + 2 * STEPS
    padded = pltpu.VMEM((high, width + 2 * PAD, depth), jnp.float32)
    plain = pltpu.VMEM((high, width, depth), jnp.float32)
    return [padded, padded, padded, plain, padded, plain, plain]


def four_steps(where, slabs, up_1, down_1, kappa, source, scratch, out):
    state, other, kappa_wide = scratch[:3]
    weights = scratch[3:7]
    rows = kappa.shape[0]
    for field in (other, kappa_wide):
        clear_edges(field)
    fill(
        kappa_wide,
        [
            (up_1, STEPS, STEPS, 0),
            (kappa, 0, rows, STEPS),
            (down_1, STEPS, STEPS, STEPS + rows),
        ],
    )
    face_weights(kappa_wide, weights, ALONG_THIRD)

    def heat(row, end):
        if row < STEPS:
            return up_1[2 * STEPS + row - 1 : 2 * STEPS + end - 1]
        if row < STEPS + rows:
            return source[row - STEPS : end - STEPS]
        return down_1[STEPS + row - rows : STEPS + end - rows]

    inside = inside_of(where[1], slabs, STEPS, rows)
    src, dst = state, other
    for step in range(1, STEPS + 1):
        count = rows + 2 * (STEPS - step)
        sweep(
            src, dst, weights, heat, step, count, 0, inside, out if step == STEPS else None
        )
        src, dst = dst, src


def first_ends_kernel(where, guess, initial, kappa, source, first_out, last_out):
    rows = kappa.shape[0]
    start = where[0] == 15
    for out, at, heat in ((first_out, 0, 0), (last_out, rows - STEPS, rows - STEPS + 1)):

        @pl.when(start)
        def _(out=out, at=at):
            out[:STEPS] = initial[at : at + STEPS]

        @pl.when(jnp.logical_not(start))
        def _(out=out, at=at):
            out[:STEPS] = guess[at : at + STEPS]

        out[STEPS : 2 * STEPS] = kappa[at : at + STEPS]
        out[2 * STEPS :] = source[heat : heat + STEPS - 1]


def phase_one_kernel(
    slabs, where, up_1, down_1, guess, initial, kappa, source, kappa_c,
    state_out, first_out, last_out, *scratch,
):
    state = scratch[0]
    rows = kappa.shape[0]
    clear_edges(state)
    fill(state, [(up_1, 0, STEPS, 0), (down_1, 0, STEPS, STEPS + rows)])

    @pl.when(where[0] == 15)
    def _():
        fill(state, [(initial, 0, rows, STEPS)])

    @pl.when(where[0] != 15)
    def _():
        fill(state, [(guess, 0, rows, STEPS)])

    def out(rows, value):
        state_out[rows] = value

    four_steps(where, slabs, up_1, down_1, kappa, source, scratch, out)

    @pl.when(where[0] == 14)
    def _():
        state_out[...] = initial[...]

    first_out[:STEPS] = state_out[:STEPS]
    last_out[:STEPS] = state_out[rows - STEPS :]
    half = kappa_c.shape[1]
    for row in range(rows // 2):
        at = (STEPS + row // 2, slice(row % 2 * half, (row % 2 + 1) * half))
        first_out[at] = kappa_c[row]
        last_out[at] = kappa_c[row]


def phase_two_kernel(
    slabs, where, up_1, down_1, up_2, down_2, before, initial, kappa, source,
    second_out, first_out, last_out, *scratch,
):
    state = scratch[0]
    rows = kappa.shape[0]
    clear_edges(state)
    fill(
        state,
        [
            (up_2, 0, STEPS, 0),
            (before, 0, rows, STEPS),
            (down_2, 0, STEPS, STEPS + rows),
        ],
    )

    def out(rows, value):
        second_out[rows] = value

    four_steps(where, slabs, up_1, down_1, kappa, source, scratch, out)

    @pl.when(where[0] == 13)
    def _():
        first_out[:STEPS] = initial[:STEPS]
        last_out[:STEPS] = initial[rows - STEPS :]

    @pl.when(where[0] != 13)
    def _():
        first_out[:STEPS] = second_out[:STEPS]
        last_out[:STEPS] = second_out[rows - STEPS :]

    first_out[STEPS:] = down_2[STEPS:]
    last_out[STEPS:] = up_2[STEPS:]


def coarse_kappa_4(field, up_2, down_2, kappa_c, at):
    block, half = kappa_c.shape[:2]
    clear_edges(field)
    fill(field, [(kappa_c, 0, block, at + block)])
    for row in range(block):
        piece = (STEPS + row // 2, slice(row % 2 * half, (row % 2 + 1) * half))
        field[at + row, PAD : PAD + half] = up_2[piece]
        field[at + 2 * block + row, PAD : PAD + half] = down_2[piece]


def coarse_scratch(rows, width, depth, fields):
    padded = pltpu.VMEM((rows, width + 2 * PAD, depth), jnp.float32)
    plain = pltpu.VMEM((rows, width, depth), jnp.float32)
    return [padded] * fields + [padded, plain, padded, plain, plain]


def phase_three_kernel(
    slabs, where, up_1, down_1, up_2, down_2, up_3, down_3, second, initial, kappa,
    source, kappa_c, second_near, third_out, tau_out, cross_out, *scratch,
):
    state, other = scratch[:2]
    base, spare, kappa_wide, *weights = scratch[7:14]
    pair = scratch[14]
    rows, width = kappa.shape[:2]
    block, half = kappa_c.shape[:2]
    clear_edges(state)
    fill(state, [(up_3, 0, STEPS, 0), (down_3, 0, STEPS, STEPS + rows)])

    @pl.when(where[0] == 13)
    def _():
        fill(state, [(initial, 0, rows, STEPS)])

    @pl.when(where[0] != 13)
    def _():
        fill(state, [(second, 0, rows, STEPS)])

    clear_edges(base)
    for row in range(block + 2):
        fine_row = STEPS - 2 + 2 * row
        pair[...] = (
            state[fine_row, PAD : PAD + width] + state[fine_row + 1, PAD : PAD + width]
        )
        base[row, PAD : PAD + half] = 0.25 * (
            pair[pl.ds(0, half, stride=2), :] + pair[pl.ds(1, half, stride=2), :]
        )

    def out(rows, value):
        third_out[rows] = value

    four_steps(where, slabs, up_1, down_1, kappa, source, scratch, out)

    @pl.when(lax.rem(where[0], GROUP) < 2)
    def _():
        cross_out[...] = second_near[...]

    @pl.when(lax.rem(where[0], GROUP) >= 2)
    def _():
        cross_out[...] = third_out[...]

    coarse_kappa_4(kappa_wide, up_2, down_2, kappa_c, 0)
    face_weights(kappa_wide, weights, 4.0 * ALONG_THIRD)

    def keep(rows, value):
        tau_out[rows] = value

    sweep(base, spare, weights, None, 1, block, block - 1, lambda row: (0, None), keep)
    use = jnp.where(where[0] == 13, 0.0, 1.0)
    for row in range(block):
        pair[...] = third_out[2 * row] + third_out[2 * row + 1]
        now = 0.25 * (
            pair[pl.ds(0, half, stride=2), :] + pair[pl.ds(1, half, stride=2), :]
        )
        tau_out[row] = now - use * tau_out[row]


def near_sums_kernel(
    slabs, where, got_3, got_2, got_1, tau, up_2, down_2, kappa_c, both_out, *scratch
):
    ahead, wrapped, spare, kappa_wide, *weights = scratch
    block, half = kappa_c.shape[:2]
    local = lax.rem(where[0], GROUP)
    high = where[0] >= GROUP
    for field in (ahead, wrapped, spare):
        clear_edges(field)
    coarse_kappa_4(kappa_wide, up_2, down_2, kappa_c, 0)
    face_weights(kappa_wide, weights, 4.0 * ALONG_THIRD)
    inside = inside_of(where[1], slabs, block, block)
    for is_ahead in (True, False):
        src, dst = (ahead, spare) if is_ahead else (wrapped, spare)
        for distance, got in ((3, got_3), (2, got_2), (1, got_1)):
            apart = high & (local >= 5) & (local < distance + 5)
            use = (local >= distance) & ~apart if is_ahead else local < distance
            use = jnp.where(use, 1.0, 0.0)
            for row in range(block + 2 * distance):
                at = (row + block - distance, slice(PAD, PAD + half))
                value = use * got[row]
                src[at] = value if distance == 3 else src[at] + value
            if distance == 1:

                def out(rows, value, is_ahead=is_ahead):
                    if is_ahead:
                        both_out[0, rows] = value + tau[rows]
                    else:
                        both_out[1, rows] = value

            else:
                out = None
            sweep(
                src, dst, weights, None, block - distance + 1, block + 2 * distance - 2,
                0, inside, out,
            )
            src, dst = dst, src


def far_sums_kernel(
    slabs, where, got_up, got, got_down, both, up_2, down_2, kappa_c, _,
    ahead_out, wrapped_out, last_out, *scratch,
):
    field, spare, kappa_wide, *weights = scratch
    block, half = kappa_c.shape[:2]
    local = lax.rem(where[0], GROUP)
    high = where[0] >= GROUP
    clear_edges(field)
    clear_edges(spare)
    coarse_kappa_4(kappa_wide, up_2, down_2, kappa_c, 0)
    face_weights(kappa_wide, weights, 4.0 * ALONG_THIRD)
    inside = inside_of(where[1], slabs, block, block)
    late = local >= 4
    to_ahead = jnp.where(late & ~(high & (local >= 5)), 1.0, 0.0)
    from_wrapped = jnp.where(late, 1.0, 0.0)
    from_ahead = jnp.where(late | (high & (local == 0)), 0.0, 1.0)
    for index, result in ((0, ahead_out), (1, wrapped_out)):
        for piece, ref in enumerate((got_up, got, got_down)):
            for row in range(block):
                at = (piece * block + row, slice(PAD, PAD + half))
                if index == 0:
                    field[at] = to_ahead * ref[0, row]
                else:
                    field[at] = from_wrapped * ref[1, row] + from_ahead * ref[0, row]

        def out(rows, value, index=index, result=result):
            result[rows] = value + both[index, rows]

        src, dst = field, spare
        for step in range(1, block + 1):
            count = 3 * block - 2 * step
            sweep(
                src, dst, weights, None, step, count, 0, inside,
                out if step == block else None,
            )
            src, dst = dst, src
    hand_wrapped = high & (local < 5)

    @pl.when(hand_wrapped)
    def _():
        last_out[...] = wrapped_out[...]

    @pl.when(jnp.logical_not(hand_wrapped))
    def _():
        last_out[...] = ahead_out[...]


def hand_over_kernel(
    slabs, where, far_up, near_up, last, near_down, far_down, up_2, down_2, up_3, down_3,
    kappa_c, ahead, wrapped, handed_out, kept_out, *scratch,
):
    field, spare, kappa_wide, *weights = scratch
    block, half = kappa_c.shape[:2]
    local = lax.rem(where[0], GROUP)
    high = where[0] >= GROUP
    clear_edges(field)
    clear_edges(spare)
    coarse_kappa_4(kappa_wide, up_2, down_2, kappa_c, block)
    for row in range(block):
        piece = (STEPS + row // 2, slice(row % 2 * half, (row % 2 + 1) * half))
        kappa_wide[row, PAD : PAD + half] = up_3[piece]
        kappa_wide[4 * block + row, PAD : PAD + half] = down_3[piece]
    fill(
        field,
        [
            (far_up, 0, block, 0),
            (near_up, 0, block, block),
            (last, 0, block, 2 * block),
            (near_down, 0, block, 3 * block),
            (far_down, 0, block, 4 * block),
        ],
    )
    face_weights(kappa_wide, weights, 4.0 * ALONG_THIRD)
    inside = inside_of(where[1], slabs, 2 * block, block)
    early = local < 5

    def one(use):
        return jnp.where(use, 1.0, 0.0)

    hand_image = one(early & ~high)
    hand_wrapped = one(early)
    hand_ahead = one(~early)
    keep_image = one(high)
    keep_wrapped = one(high & ~early)
    keep_ahead = one(early)

    def out(rows, value):
        a, w = ahead[rows], wrapped[rows]
        handed_out[rows] = hand_image * value + hand_wrapped * w + hand_ahead * a
        kept_out[rows] = keep_image * value + keep_wrapped * w + keep_ahead * a

    src, dst = field, spare
    for step in range(1, 2 * block + 1):
        count = 5 * block - 2 * step
        sweep(
            src, dst, weights, None, step, count, 0, inside,
            out if step == 2 * block else None,
        )
        src, dst = dst, src


def call(kernel, slabs, outs, scratch, where, *args, unread=0):
    vmem = pl.BlockSpec(memory_space=pltpu.VMEM)
    anywhere = pl.BlockSpec(memory_space=pl.ANY)
    return pl.pallas_call(
        kernel if slabs is None else functools.partial(kernel, slabs),
        out_shape=[jax.ShapeDtypeStruct(shape, jnp.float32) for shape in outs],
        in_specs=[pl.BlockSpec(memory_space=pltpu.SMEM)]
        + [vmem] * (len(args) - unread)
        + [anywhere] * unread,
        out_specs=[vmem] * len(outs),
        scratch_shapes=scratch,
        compiler_params=pltpu.CompilerParams(vmem_limit_bytes=40 * 2**20),
        cost_estimate=pl.CostEstimate(flops=0, bytes_accessed=0, transcendentals=0),
    )(where, *args)


def per_device(initial, guess, conductivity, source):
    rows, width_two, width_three = conductivity.shape
    crows, half = rows // 2, width_two // 2
    slabs = lax.axis_size("space")
    tm = lax.axis_index("tm")
    sp = lax.axis_index("space")
    local = tm % GROUP
    where = jnp.stack([tm, sp]).astype(jnp.int32)

    def cut(array, have, want):
        return array[have - want : array.shape[0] - (have - want)]

    def route(block, pairs):
        return lax.ppermute(block, ("tm", "space"), pairs)

    def along_space(block, distance):
        pairs = [
            (i, i + distance) for i in range(slabs) if 0 <= i + distance < slabs
        ]
        return lax.ppermute(block, "space", pairs)

    def along_time(block, pairs):
        return lax.ppermute(block, "tm", pairs)

    def ring(shift):
        return [
            (g * GROUP + i, g * GROUP + (i + shift) % GROUP)
            for g in (0, 1)
            for i in range(GROUP)
        ]

    def restrict(field):
        return field.reshape(-1, 2, half, 2, width_three).mean(axis=(1, 3))

    def neighbours(block_first, block_last):
        return along_space(block_last, 1), along_space(block_first, -1)

    block_shape = (rows, width_two, width_three)
    coarse_shape = (crows, half, width_three)
    packed_shape = (STEPS + crows // 2, width_two, width_three)
    scratch = fine_scratch(rows, width_two, width_three)

    kappa_c = restrict(conductivity)
    first, last = call(
        first_ends_kernel, None, [(3 * STEPS - 1, width_two, width_three)] * 2, [],
        where, guess[0], initial, conductivity, source,
    )
    sides = neighbours(first, last)
    state, first, last = call(
        phase_one_kernel, slabs, [block_shape, packed_shape, packed_shape], scratch,
        where, *sides, guess[0], initial, conductivity, source, kappa_c,
    )
    sides_2 = neighbours(first, last)
    second, first, last = call(
        phase_two_kernel, slabs, [block_shape, packed_shape, packed_shape], scratch,
        where, *sides, *sides_2, state, initial, conductivity, source,
    )
    sides_3 = neighbours(first, last)
    second_near = along_time(second, ring(2))
    third, tau, crossed = call(
        phase_three_kernel, slabs, [block_shape, coarse_shape, block_shape],
        scratch
        + coarse_scratch(3 * crows, half, width_three, 2)
        + [pltpu.VMEM((width_two, width_three), jnp.float32)],
        where, *sides, *sides_2, *sides_3, second, initial, conductivity, source, kappa_c,
        second_near,
    )

    up, down = neighbours(tau, tau)
    tau_wide = jnp.concatenate([up, tau, down], 0)
    sent = [cut(tau_wide, crows, d) for d in (3, 2, 1)]
    got = [along_time(block, ring(d)) for d, block in zip((3, 2, 1), sent)]
    crossed = along_time(
        lax.optimization_barrier((crossed, got[2]))[0],
        [(i, i ^ GROUP) for i in range(2 * GROUP) if i % GROUP in (0, 1, 5, 6, 7)],
    )
    (both,) = call(
        near_sums_kernel, slabs, [(2,) + coarse_shape],
        coarse_scratch(3 * crows, half, width_three, 3),
        where, *got, tau, *sides_2, kappa_c,
    )

    def diagonal(distance):
        pairs = [
            (t * slabs + i, u * slabs + i + distance)
            for t, u in ring(4)
            for i in range(slabs)
            if 0 <= i + distance < slabs
        ]
        return route(both, pairs)

    got = [diagonal(1), diagonal(0), diagonal(-1)]
    ahead, wrapped, last = call(
        far_sums_kernel, slabs, [coarse_shape] * 3,
        coarse_scratch(3 * crows, half, width_three, 2),
        where, *got, both, *sides_2, kappa_c, crossed, unread=1,
    )

    third_home = along_time(
        lax.optimization_barrier((jnp.where(local >= 5, crossed, third), last))[0],
        ring(3),
    )
    near = neighbours(last, last)
    far = (along_space(last, 2), along_space(last, -2))
    handed, kept = call(
        hand_over_kernel, slabs, [coarse_shape] * 2,
        coarse_scratch(5 * crows, half, width_three, 2),
        where, far[0], near[0], last, near[1], far[1], *sides_2, *sides_3, kappa_c,
        ahead, wrapped,
    )
    handed = along_time(
        handed,
        [
            (g * GROUP + i, (1 - g) * GROUP + (i + 3) % GROUP)
            for g in (0, 1)
            for i in range(GROUP)
        ],
    )
    kept = along_time(kept, ring(3))
    second_home = jnp.where(local < 2, crossed, second_near)

    residual = third_home - second_home
    change = handed + kept - restrict(second_home)
    finer = jnp.repeat(jnp.repeat(change, 2, axis=0), 2, axis=1)
    corrected = second_home + finer
    return (corrected[None], residual[None])


def solution(mesh):
    in_specs = (
        P("space", None, None),
        P("tm", "space", None, None),
        P("space", None, None),
        P("space", None, None),
    )
    out_specs = (P("tm", "space", None, None), P("tm", "space", None, None))
    return jax.shard_map(
        per_device, mesh=mesh, in_specs=in_specs, out_specs=out_specs, check_vma=False
    )
```

```python
import functools

import jax
import jax.numpy as jnp
from jax import lax
from jax.experimental import pallas as pl
from jax.experimental.pallas import tpu as pltpu
from jax.sharding import PartitionSpec as P

STEPS = 4
ALONG_FIRST = 0.1
ALONG_SECOND = 0.1
ALONG_THIRD = 0.0125
GROUP = 8
PAD = 8


def lane_mask(shape, *lanes):
    lane = lax.broadcasted_iota(jnp.int32, shape, 1)
    hit = lane == lanes[0]
    for other in lanes[1:]:
        hit = hit | (lane == other)
    return hit


def clear_edges(field):
    rows, wide, depth = field.shape
    zero = jnp.zeros((rows, PAD, depth), jnp.float32)
    field[:, :PAD] = zero
    field[:, wide - PAD :] = zero


def face_weights(kappa, weights, third):
    by_first, by_second, by_third, keep = weights
    rows, wide, depth = kappa.shape
    width = wide - 2 * PAD
    first_w, third_w = 0.5 * ALONG_FIRST, 0.5 * third
    inner = slice(PAD, PAD + width)
    for row in range(rows):
        k = kappa[row, inner]
        if row:
            by_first[row] = first_w * (kappa[row - 1, inner] + k)
        by_second[row, inner] = first_w * (kappa[row, PAD - 1 : PAD - 1 + width] + k)
        by_second[row, PAD + width :] = (
            first_w * kappa[row, PAD + width - 1 : 2 * PAD + width - 1]
        )
        deeper = pltpu.roll(k, depth - 1, 1)
        by_third[row] = jnp.where(
            lane_mask(k.shape, depth - 1), 0.0, third_w * (k + deeper)
        )
        keep[row] = jnp.where(lane_mask(k.shape, 0, depth - 1), 1.0 - third_w * k, 1.0)


def sweep(src, dst, weights, heat, first, count, shift, inside, out=None):
    by_first, by_second, by_third, keep = weights
    wide, depth = src.shape[1:]
    width = wide - 2 * PAD
    most = max(1, 256 // width)
    inner = slice(PAD, PAD + width)
    upper = slice(PAD + 1, PAD + 1 + width)
    lower = slice(PAD - 1, PAD - 1 + width)
    row = first
    while row < first + count:
        key, mask = inside(row)
        end = row + 1
        while end < first + count and end - row < most and inside(end)[0] == key:
            end += 1
        here = slice(row, end)
        w = slice(row + shift, end + shift)
        v = src[here, inner]
        total = by_first[row + shift + 1 : end + shift + 1] * (
            src[row + 1 : end + 1, inner] - v
        ) - by_first[w] * (v - src[row - 1 : end - 1, inner])
        total = total + (
            by_second[w, upper] * (src[here, upper] - v)
            - by_second[w, inner] * (v - src[here, lower])
        )
        deep = by_third[w] * (pltpu.roll(v, depth - 1, 2) - v)
        total = keep[w] * v + (total + (deep - pltpu.roll(deep, 1, 2)))
        if heat is not None:
            total = total + heat(row, end)
        if mask is not None:
            total = total * mask
        if out is None:
            dst[here, inner] = total
        else:
            out(slice(row - first, end - first), total)
        row = end


def inside_of(place, slabs, margin, block):
    def inside(row):
        if row < margin:
            need = (margin - row + block - 1) // block
            return -need, jnp.where(place >= need, 1.0, 0.0)
        if row >= margin + block:
            need = (row - margin) // block
            return need, jnp.where(place + need < slabs, 1.0, 0.0)
        return 0, None

    return inside


def fill(field, pieces):
    width = field.shape[1] - 2 * PAD
    for ref, first, count, row in pieces:
        field[row : row + count, PAD : PAD + width] = ref[first : first + count]


def fine_scratch(rows, width, depth):
    high = rows + 2 * STEPS
    padded = pltpu.VMEM((high, width + 2 * PAD, depth), jnp.float32)
    plain = pltpu.VMEM((high, width, depth), jnp.float32)
    return [padded, padded, padded, plain, padded, plain, plain]


def four_steps(where, slabs, up_1, down_1, kappa, source, scratch, out):
    state, other, kappa_wide = scratch[:3]
    weights = scratch[3:7]
    rows = kappa.shape[0]
    for field in (other, kappa_wide):
        clear_edges(field)
    fill(
        kappa_wide,
        [
            (up_1, STEPS, STEPS, 0),
            (kappa, 0, rows, STEPS),
            (down_1, STEPS, STEPS, STEPS + rows),
        ],
    )
    face_weights(kappa_wide, weights, ALONG_THIRD)

    def heat(row, end):
        if row < STEPS:
            return up_1[2 * STEPS + row - 1 : 2 * STEPS + end - 1]
        if row < STEPS + rows:
            return source[row - STEPS : end - STEPS]
        return down_1[STEPS + row - rows : STEPS + end - rows]

    inside = inside_of(where[1], slabs, STEPS, rows)
    src, dst = state, other
    for step in range(1, STEPS + 1):
        count = rows + 2 * (STEPS - step)
        sweep(
            src, dst, weights, heat, step, count, 0, inside, out if step == STEPS else None
        )
        src, dst = dst, src


def first_ends_kernel(
    where, guess, initial, kappa, source, first_out, last_out, sems
):
    rows = kappa.shape[0]

    def copies(state):
        index = 0
        for out, at, heat in (
            (first_out, 0, 0),
            (last_out, rows - STEPS, rows - STEPS + 1),
        ):
            for ref, first, count, row in (
                (state, at, STEPS, 0),
                (kappa, at, STEPS, STEPS),
                (source, heat, STEPS - 1, 2 * STEPS),
            ):
                yield pltpu.make_async_copy(
                    ref.at[pl.ds(first, count)], out.at[pl.ds(row, count)], sems.at[index]
                )
                index += 1

    @pl.when(where[0] == 15)
    def _():
        for copy in copies(initial):
            copy.start()
        for copy in copies(initial):
            copy.wait()

    @pl.when(where[0] != 15)
    def _():
        for copy in copies(guess):
            copy.start()
        for copy in copies(guess):
            copy.wait()


def phase_one_kernel(
    slabs, where, up_1, down_1, guess, initial, kappa, source, kappa_c,
    state_out, first_out, last_out, *scratch,
):
    state = scratch[0]
    rows = kappa.shape[0]
    clear_edges(state)
    fill(state, [(up_1, 0, STEPS, 0), (down_1, 0, STEPS, STEPS + rows)])

    @pl.when(where[0] == 15)
    def _():
        fill(state, [(initial, 0, rows, STEPS)])

    @pl.when(where[0] != 15)
    def _():
        fill(state, [(guess, 0, rows, STEPS)])

    def out(rows, value):
        state_out[rows] = value

    four_steps(where, slabs, up_1, down_1, kappa, source, scratch, out)

    @pl.when(where[0] == 14)
    def _():
        state_out[...] = initial[...]

    first_out[:STEPS] = state_out[:STEPS]
    last_out[:STEPS] = state_out[rows - STEPS :]
    half = kappa_c.shape[1]
    for row in range(rows // 2):
        at = (STEPS + row // 2, slice(row % 2 * half, (row % 2 + 1) * half))
        first_out[at] = kappa_c[row]
        last_out[at] = kappa_c[row]


def phase_two_kernel(
    slabs, where, up_1, down_1, up_2, down_2, before, initial, kappa, source,
    second_out, first_out, last_out, *scratch,
):
    state = scratch[0]
    rows = kappa.shape[0]
    clear_edges(state)
    fill(
        state,
        [
            (up_2, 0, STEPS, 0),
            (before, 0, rows, STEPS),
            (down_2, 0, STEPS, STEPS + rows),
        ],
    )

    def out(rows, value):
        second_out[rows] = value

    four_steps(where, slabs, up_1, down_1, kappa, source, scratch, out)

    @pl.when(where[0] == 13)
    def _():
        first_out[:STEPS] = initial[:STEPS]
        last_out[:STEPS] = initial[rows - STEPS :]

    @pl.when(where[0] != 13)
    def _():
        first_out[:STEPS] = second_out[:STEPS]
        last_out[:STEPS] = second_out[rows - STEPS :]

    first_out[STEPS:] = down_2[STEPS:]
    last_out[STEPS:] = up_2[STEPS:]


def coarse_kappa_4(field, up_2, down_2, kappa_c, at):
    block, half = kappa_c.shape[:2]
    clear_edges(field)
    fill(field, [(kappa_c, 0, block, at + block)])
    for row in range(block):
        piece = (STEPS + row // 2, slice(row % 2 * half, (row % 2 + 1) * half))
        field[at + row, PAD : PAD + half] = up_2[piece]
        field[at + 2 * block + row, PAD : PAD + half] = down_2[piece]


def coarse_scratch(rows, width, depth, fields):
    padded = pltpu.VMEM((rows, width + 2 * PAD, depth), jnp.float32)
    plain = pltpu.VMEM((rows, width, depth), jnp.float32)
    return [padded] * fields + [padded, plain, padded, plain, plain]


def phase_three_kernel(
    slabs, where, up_1, down_1, up_2, down_2, up_3, down_3, second, initial, kappa,
    source, kappa_c, second_near, third_out, tau_out, cross_out, *scratch,
):
    state, other = scratch[:2]
    base, spare, kappa_wide, *weights = scratch[7:14]
    pair = scratch[14]
    rows, width = kappa.shape[:2]
    block, half = kappa_c.shape[:2]
    clear_edges(state)
    fill(state, [(up_3, 0, STEPS, 0), (down_3, 0, STEPS, STEPS + rows)])

    @pl.when(where[0] == 13)
    def _():
        fill(state, [(initial, 0, rows, STEPS)])

    @pl.when(where[0] != 13)
    def _():
        fill(state, [(second, 0, rows, STEPS)])

    clear_edges(base)
    for row in range(block + 2):
        fine_row = STEPS - 2 + 2 * row
        pair[...] = (
            state[fine_row, PAD : PAD + width] + state[fine_row + 1, PAD : PAD + width]
        )
        base[row, PAD : PAD + half] = 0.25 * (
            pair[pl.ds(0, half, stride=2), :] + pair[pl.ds(1, half, stride=2), :]
        )

    def out(rows, value):
        third_out[rows] = value

    four_steps(where, slabs, up_1, down_1, kappa, source, scratch, out)

    @pl.when(lax.rem(where[0], GROUP) < 2)
    def _():
        cross_out[...] = second_near[...]

    @pl.when(lax.rem(where[0], GROUP) >= 2)
    def _():
        cross_out[...] = third_out[...]

    coarse_kappa_4(kappa_wide, up_2, down_2, kappa_c, 0)
    face_weights(kappa_wide, weights, 4.0 * ALONG_THIRD)

    def keep(rows, value):
        tau_out[rows] = value

    sweep(base, spare, weights, None, 1, block, block - 1, lambda row: (0, None), keep)
    use = jnp.where(where[0] == 13, 0.0, 1.0)
    for row in range(block):
        pair[...] = third_out[2 * row] + third_out[2 * row + 1]
        now = 0.25 * (
            pair[pl.ds(0, half, stride=2), :] + pair[pl.ds(1, half, stride=2), :]
        )
        tau_out[row] = now - use * tau_out[row]


def coarse_kappa_8(field, up_2, down_2, up_3, down_3, kappa_c):
    block, half = kappa_c.shape[:2]
    coarse_kappa_4(field, up_2, down_2, kappa_c, block)
    for row in range(block):
        piece = (STEPS + row // 2, slice(row % 2 * half, (row % 2 + 1) * half))
        field[row, PAD : PAD + half] = up_3[piece]
        field[4 * block + row, PAD : PAD + half] = down_3[piece]


def far_sums_kernel(
    slabs, where, got_a, got_b, wide_a, wide_b, up_2, down_2, up_3, down_3, kappa_c,
    ahead_out, wrapped_out, *scratch,
):
    field, spare, kappa_wide, *weights = scratch
    block = kappa_c.shape[0]
    deep = 2 * block - 1
    rows = block + 2 * deep
    part = rows // 2
    local = lax.rem(where[0], GROUP)
    high = where[0] >= GROUP
    clear_edges(field)
    clear_edges(spare)
    coarse_kappa_8(kappa_wide, up_2, down_2, up_3, down_3, kappa_c)
    face_weights(kappa_wide, weights, 4.0 * ALONG_THIRD)
    fill(field, [(got_a, 1, part, 0), (got_b, 0, part, part)])
    inside = inside_of(where[1], slabs, deep, block)
    late = local >= 4
    to_ahead = jnp.where(late & ~(high & (local >= 5)), 1.0, 0.0)
    to_wrapped = jnp.where(late | (high & (local == 0)), 0.0, 1.0)

    def out(rows, value):
        ahead_out[rows] = to_ahead * value
        wrapped_out[rows] = to_wrapped * value

    src, dst = field, spare
    for step in range(1, block + 1):
        sweep(
            src, dst, weights, None, step, rows - 2 * step, 1, inside,
            out if step == block else None,
        )
        src, dst = dst, src
    cut = part - block
    ahead_out[:cut] = ahead_out[:cut] + wide_a[block + 1 :]
    ahead_out[cut:] = ahead_out[cut:] + wide_b[: rows - 2 * block - cut]


def near_sums_kernel(
    slabs, where, got_3, got_2, got_1, behind_3, behind_2, behind_1, own_ahead,
    own_wrapped, up_2, down_2, kappa_c, ahead_out, wrapped_out, last_out, *scratch,
):
    ahead, wrapped, spare, kappa_wide, *weights = scratch
    block, half = kappa_c.shape[:2]
    local = lax.rem(where[0], GROUP)
    high = where[0] >= GROUP
    for field in (ahead, wrapped, spare):
        clear_edges(field)
    coarse_kappa_4(kappa_wide, up_2, down_2, kappa_c, 0)
    face_weights(kappa_wide, weights, 4.0 * ALONG_THIRD)
    inside = inside_of(where[1], slabs, block, block)
    own = slice(block - 1, 2 * block - 1)
    for is_ahead in (True, False):
        src, dst = (ahead, spare) if is_ahead else (wrapped, spare)
        for distance, got, behind in (
            (3, got_3, behind_3), (2, got_2, behind_2), (1, got_1, behind_1),
        ):
            apart = high & (local >= 5) & (local < distance + 5)
            use = (local >= distance) & ~apart if is_ahead else local < distance
            value = jnp.where(use, 1.0, 0.0) * got[...]
            if not is_ahead:
                value = value + behind[...]
            at = (
                slice(block - distance, 2 * block + distance),
                slice(PAD, PAD + half),
            )
            src[at] = value if distance == 3 else src[at] + value
            if distance == 1:

                def out(rows, value, is_ahead=is_ahead):
                    result, mine = (
                        (ahead_out, own_ahead) if is_ahead else (wrapped_out, own_wrapped)
                    )
                    result[rows] = value + mine[own][rows]

            else:
                out = None
            sweep(
                src, dst, weights, None, block - distance + 1, block + 2 * distance - 2,
                0, inside, out,
            )
            src, dst = dst, src
    hand_wrapped = high & (local < 5)

    @pl.when(hand_wrapped)
    def _():
        last_out[...] = wrapped_out[...]

    @pl.when(jnp.logical_not(hand_wrapped))
    def _():
        last_out[...] = ahead_out[...]


def hand_over_kernel(
    slabs, where, far_up, near_up, last, near_down, far_down, up_2, down_2, up_3, down_3,
    kappa_c, ahead, wrapped, _, handed_out, kept_out, *scratch,
):
    field, spare, kappa_wide, *weights = scratch
    block, half = kappa_c.shape[:2]
    local = lax.rem(where[0], GROUP)
    high = where[0] >= GROUP
    clear_edges(field)
    clear_edges(spare)
    coarse_kappa_8(kappa_wide, up_2, down_2, up_3, down_3, kappa_c)
    fill(
        field,
        [
            (far_up, 0, block, 0),
            (near_up, 0, block, block),
            (last, 0, block, 2 * block),
            (near_down, 0, block, 3 * block),
            (far_down, 0, block, 4 * block),
        ],
    )
    face_weights(kappa_wide, weights, 4.0 * ALONG_THIRD)
    inside = inside_of(where[1], slabs, 2 * block, block)
    early = local < 5

    def one(use):
        return jnp.where(use, 1.0, 0.0)

    hand_image = one(early & ~high)
    hand_wrapped = one(early)
    hand_ahead = one(~early)
    keep_image = one(high)
    keep_wrapped = one(high & ~early)
    keep_ahead = one(early)

    def out(rows, value):
        a, w = ahead[rows], wrapped[rows]
        handed_out[rows] = hand_image * value + hand_wrapped * w + hand_ahead * a
        kept_out[rows] = keep_image * value + keep_wrapped * w + keep_ahead * a

    src, dst = field, spare
    for step in range(1, 2 * block + 1):
        count = 5 * block - 2 * step
        sweep(
            src, dst, weights, None, step, count, 0, inside,
            out if step == 2 * block else None,
        )
        src, dst = dst, src


def call(kernel, slabs, outs, scratch, where, *args, unread=0, room=40):
    vmem = pl.BlockSpec(memory_space=pltpu.VMEM)
    anywhere = pl.BlockSpec(memory_space=pl.ANY)
    return pl.pallas_call(
        kernel if slabs is None else functools.partial(kernel, slabs),
        out_shape=[jax.ShapeDtypeStruct(shape, jnp.float32) for shape in outs],
        in_specs=[pl.BlockSpec(memory_space=pltpu.SMEM)]
        + [vmem] * (len(args) - unread)
        + [anywhere] * unread,
        out_specs=[vmem] * len(outs),
        scratch_shapes=scratch,
        compiler_params=pltpu.CompilerParams(vmem_limit_bytes=room * 2**20),
        cost_estimate=pl.CostEstimate(flops=0, bytes_accessed=0, transcendentals=0),
    )(where, *args)


def per_device(initial, guess, conductivity, source):
    rows, width_two, width_three = conductivity.shape
    crows, half = rows // 2, width_two // 2
    slabs = lax.axis_size("space")
    tm = lax.axis_index("tm")
    sp = lax.axis_index("space")
    local = tm % GROUP
    where = jnp.stack([tm, sp]).astype(jnp.int32)

    def cut(array, have, want):
        return array[have - want : array.shape[0] - (have - want)]

    def along_space(block, distance):
        pairs = [
            (i, i + distance) for i in range(slabs) if 0 <= i + distance < slabs
        ]
        return lax.ppermute(block, "space", pairs)

    def along_time(block, pairs):
        return lax.ppermute(block, "tm", pairs)

    def ring(shift):
        return [
            (g * GROUP + i, g * GROUP + (i + shift) % GROUP)
            for g in (0, 1)
            for i in range(GROUP)
        ]

    def restrict(field):
        return field.reshape(-1, 2, half, 2, width_three).mean(axis=(1, 3))

    def neighbours(block_first, block_last):
        return along_space(block_last, 1), along_space(block_first, -1)

    block_shape = (rows, width_two, width_three)
    coarse_shape = (crows, half, width_three)
    packed_shape = (STEPS + crows // 2, width_two, width_three)
    scratch = fine_scratch(rows, width_two, width_three)

    kappa_c = restrict(conductivity)
    first, last = call(
        first_ends_kernel, None, [(3 * STEPS - 1, width_two, width_three)] * 2,
        [pltpu.SemaphoreType.DMA((6,))],
        where, guess[0], initial, conductivity, source, unread=4, room=60,
    )
    sides = neighbours(first, last)
    state, first, last = call(
        phase_one_kernel, slabs, [block_shape, packed_shape, packed_shape], scratch,
        where, *sides, guess[0], initial, conductivity, source, kappa_c,
    )
    sides_2 = neighbours(first, last)
    second, first, last = call(
        phase_two_kernel, slabs, [block_shape, packed_shape, packed_shape], scratch,
        where, *sides, *sides_2, state, initial, conductivity, source,
    )
    sides_3 = neighbours(first, last)
    second_near = along_time(second, ring(2))
    third, tau, crossed = call(
        phase_three_kernel, slabs, [block_shape, coarse_shape, block_shape],
        scratch
        + coarse_scratch(3 * crows, half, width_three, 2)
        + [pltpu.VMEM((width_two, width_three), jnp.float32)],
        where, *sides, *sides_2, *sides_3, second, initial, conductivity, source, kappa_c,
        second_near,
    )

    deep = 2 * crows - 1
    far = (along_space(tau, 2), along_space(tau, -2))
    near = neighbours(tau, tau)
    tau_wide = jnp.concatenate([far[0], near[0], tau, near[1], far[1]], 0)
    part = tau_wide.shape[0] // 2
    wide = (tau_wide[:part], tau_wide[part:])
    got_a = along_time(wide[0], ring(4))
    crossed = along_time(
        lax.optimization_barrier((crossed, got_a))[0],
        [(i, i ^ GROUP) for i in range(2 * GROUP) if i % GROUP in (0, 1, 5, 6, 7)],
    )
    got_b = along_time(wide[1], ring(4))
    wide_shape = (deep + 3,) + coarse_shape[1:]
    ahead, wrapped = call(
        far_sums_kernel, slabs, [wide_shape] * 2,
        coarse_scratch(5 * crows, half, width_three, 2),
        where, got_a, got_b, *wide, *sides_2, *sides_3, kappa_c,
    )
    behind_pairs = lambda d: [
        (g * GROUP + i, g * GROUP + i + d) for g in (0, 1) for i in range(4)
    ]
    got = [along_time(cut(ahead, 3, d), ring(d)) for d in (3, 2, 1)]
    behind = [along_time(cut(wrapped, 3, d), behind_pairs(d)) for d in (3, 2, 1)]
    ahead, wrapped, last = call(
        near_sums_kernel, slabs, [coarse_shape] * 3,
        coarse_scratch(3 * crows, half, width_three, 3),
        where, *got, *behind, ahead, wrapped, *sides_2, kappa_c,
    )

    near = neighbours(last, last)
    far = (along_space(last, 2), along_space(last, -2))
    handed, kept = call(
        hand_over_kernel, slabs, [coarse_shape] * 2,
        coarse_scratch(5 * crows, half, width_three, 2),
        where, far[0], near[0], last, near[1], far[1], *sides_2, *sides_3, kappa_c,
        ahead, wrapped, crossed, unread=1,
    )
    third = lax.optimization_barrier(
        (jnp.where(local >= 5, crossed, third), handed)
    )[0]
    handed = along_time(
        handed,
        [
            (g * GROUP + i, (1 - g) * GROUP + (i + 3) % GROUP)
            for g in (0, 1)
            for i in range(GROUP)
        ],
    )
    kept = along_time(kept, ring(3))
    third_home = along_time(third, ring(3))
    second_home = jnp.where(local < 2, crossed, second_near)

    residual = third_home - second_home
    change = handed + kept - restrict(second_home)
    finer = jnp.repeat(jnp.repeat(change, 2, axis=0), 2, axis=1)
    corrected = second_home + finer
    return (corrected[None], residual[None])


def solution(mesh):
    in_specs = (
        P("space", None, None),
        P("tm", "space", None, None),
        P("space", None, None),
        P("space", None, None),
    )
    out_specs = (P("tm", "space", None, None), P("tm", "space", None, None))
    return jax.shard_map(
        per_device, mesh=mesh, in_specs=in_specs, out_specs=out_specs, check_vma=False
    )
```

```python
import functools

import jax
import jax.numpy as jnp
from jax import lax
from jax.experimental import pallas as pl
from jax.experimental.pallas import tpu as pltpu
from jax.sharding import PartitionSpec as P

STEPS = 4
ALONG_FIRST = 0.1
ALONG_SECOND = 0.1
ALONG_THIRD = 0.0125
GROUP = 8
PAD = 8


def lane_mask(shape, *lanes):
    lane = lax.broadcasted_iota(jnp.int32, shape, 1)
    hit = lane == lanes[0]
    for other in lanes[1:]:
        hit = hit | (lane == other)
    return hit


def clear_edges(field):
    rows, wide, depth = field.shape
    zero = jnp.zeros((rows, PAD, depth), jnp.float32)
    field[:, :PAD] = zero
    field[:, wide - PAD :] = zero


def face_weights(kappa, weights, third):
    by_first, by_second, by_third, keep = weights
    rows, wide, depth = kappa.shape
    width = wide - 2 * PAD
    first_w, third_w = 0.5 * ALONG_FIRST, 0.5 * third
    inner = slice(PAD, PAD + width)
    for row in range(rows):
        k = kappa[row, inner]
        if row:
            by_first[row] = first_w * (kappa[row - 1, inner] + k)
        by_second[row, inner] = first_w * (kappa[row, PAD - 1 : PAD - 1 + width] + k)
        by_second[row, PAD + width :] = (
            first_w * kappa[row, PAD + width - 1 : 2 * PAD + width - 1]
        )
        deeper = pltpu.roll(k, depth - 1, 1)
        by_third[row] = jnp.where(
            lane_mask(k.shape, depth - 1), 0.0, third_w * (k + deeper)
        )
        keep[row] = jnp.where(lane_mask(k.shape, 0, depth - 1), 1.0 - third_w * k, 1.0)


def sweep(src, dst, weights, heat, first, count, shift, inside, out=None):
    by_first, by_second, by_third, keep = weights
    wide, depth = src.shape[1:]
    width = wide - 2 * PAD
    most = max(1, 256 // width)
    inner = slice(PAD, PAD + width)
    upper = slice(PAD + 1, PAD + 1 + width)
    lower = slice(PAD - 1, PAD - 1 + width)
    row = first
    while row < first + count:
        key, mask = inside(row)
        end = row + 1
        while end < first + count and end - row < most and inside(end)[0] == key:
            end += 1
        here = slice(row, end)
        w = slice(row + shift, end + shift)
        v = src[here, inner]
        total = by_first[row + shift + 1 : end + shift + 1] * (
            src[row + 1 : end + 1, inner] - v
        ) - by_first[w] * (v - src[row - 1 : end - 1, inner])
        total = total + (
            by_second[w, upper] * (src[here, upper] - v)
            - by_second[w, inner] * (v - src[here, lower])
        )
        deep = by_third[w] * (pltpu.roll(v, depth - 1, 2) - v)
        total = keep[w] * v + (total + (deep - pltpu.roll(deep, 1, 2)))
        if heat is not None:
            total = total + heat(row, end)
        if mask is not None:
            total = total * mask
        if out is None:
            dst[here, inner] = total
        else:
            out(slice(row - first, end - first), total)
        row = end


def inside_of(place, slabs, margin, block):
    def inside(row):
        if row < margin:
            need = (margin - row + block - 1) // block
            return -need, jnp.where(place >= need, 1.0, 0.0)
        if row >= margin + block:
            need = (row - margin) // block
            return need, jnp.where(place + need < slabs, 1.0, 0.0)
        return 0, None

    return inside


def fill(field, pieces):
    width = field.shape[1] - 2 * PAD
    for ref, first, count, row in pieces:
        field[row : row + count, PAD : PAD + width] = ref[first : first + count]


def fine_scratch(rows, width, depth):
    high = rows + 2 * STEPS
    padded = pltpu.VMEM((high, width + 2 * PAD, depth), jnp.float32)
    plain = pltpu.VMEM((high, width, depth), jnp.float32)
    return [padded, padded, padded, plain, padded, plain, plain]


def four_steps(where, slabs, up_1, down_1, kappa, source, scratch, out):
    state, other, kappa_wide = scratch[:3]
    weights = scratch[3:7]
    rows = kappa.shape[0]
    for field in (other, kappa_wide):
        clear_edges(field)
    fill(
        kappa_wide,
        [
            (up_1, STEPS, STEPS, 0),
            (kappa, 0, rows, STEPS),
            (down_1, STEPS, STEPS, STEPS + rows),
        ],
    )
    face_weights(kappa_wide, weights, ALONG_THIRD)

    def heat(row, end):
        if row < STEPS:
            return up_1[2 * STEPS + row - 1 : 2 * STEPS + end - 1]
        if row < STEPS + rows:
            return source[row - STEPS : end - STEPS]
        return down_1[STEPS + row - rows : STEPS + end - rows]

    inside = inside_of(where[1], slabs, STEPS, rows)
    src, dst = state, other
    for step in range(1, STEPS + 1):
        count = rows + 2 * (STEPS - step)
        sweep(
            src, dst, weights, heat, step, count, 0, inside, out if step == STEPS else None
        )
        src, dst = dst, src


def first_ends_kernel(
    where, guess, initial, kappa, source, first_out, last_out, sems
):
    rows = kappa.shape[0]

    def copies(state):
        index = 0
        for out, at, heat in (
            (first_out, 0, 0),
            (last_out, rows - STEPS, rows - STEPS + 1),
        ):
            for ref, first, count, row in (
                (state, at, STEPS, 0),
                (kappa, at, STEPS, STEPS),
                (source, heat, STEPS - 1, 2 * STEPS),
            ):
                yield pltpu.make_async_copy(
                    ref.at[pl.ds(first, count)], out.at[pl.ds(row, count)], sems.at[index]
                )
                index += 1

    @pl.when(where[0] == 15)
    def _():
        for copy in copies(initial):
            copy.start()
        for copy in copies(initial):
            copy.wait()

    @pl.when(where[0] != 15)
    def _():
        for copy in copies(guess):
            copy.start()
        for copy in copies(guess):
            copy.wait()


def phase_one_kernel(
    slabs, where, up_1, down_1, guess, initial, kappa, source, kappa_c,
    state_out, first_out, last_out, *scratch,
):
    state = scratch[0]
    rows = kappa.shape[0]
    clear_edges(state)
    fill(state, [(up_1, 0, STEPS, 0), (down_1, 0, STEPS, STEPS + rows)])

    @pl.when(where[0] == 15)
    def _():
        fill(state, [(initial, 0, rows, STEPS)])

    @pl.when(where[0] != 15)
    def _():
        fill(state, [(guess, 0, rows, STEPS)])

    def out(rows, value):
        state_out[rows] = value

    four_steps(where, slabs, up_1, down_1, kappa, source, scratch, out)

    @pl.when(where[0] == 14)
    def _():
        state_out[...] = initial[...]

    first_out[:STEPS] = state_out[:STEPS]
    last_out[:STEPS] = state_out[rows - STEPS :]
    half = kappa_c.shape[1]
    for row in range(rows // 2):
        at = (STEPS + row // 2, slice(row % 2 * half, (row % 2 + 1) * half))
        first_out[at] = kappa_c[row]
        last_out[at] = kappa_c[row]


def phase_two_kernel(
    slabs, where, up_1, down_1, up_2, down_2, before, initial, kappa, source,
    second_out, first_out, last_out, *scratch,
):
    state = scratch[0]
    rows = kappa.shape[0]
    clear_edges(state)
    fill(
        state,
        [
            (up_2, 0, STEPS, 0),
            (before, 0, rows, STEPS),
            (down_2, 0, STEPS, STEPS + rows),
        ],
    )

    def out(rows, value):
        second_out[rows] = value

    four_steps(where, slabs, up_1, down_1, kappa, source, scratch, out)

    @pl.when(where[0] == 13)
    def _():
        first_out[:STEPS] = initial[:STEPS]
        last_out[:STEPS] = initial[rows - STEPS :]

    @pl.when(where[0] != 13)
    def _():
        first_out[:STEPS] = second_out[:STEPS]
        last_out[:STEPS] = second_out[rows - STEPS :]

    first_out[STEPS:] = down_2[STEPS:]
    last_out[STEPS:] = up_2[STEPS:]


def coarse_kappa_4(field, up_2, down_2, kappa_c, at):
    block, half = kappa_c.shape[:2]
    clear_edges(field)
    fill(field, [(kappa_c, 0, block, at + block)])
    for row in range(block):
        piece = (STEPS + row // 2, slice(row % 2 * half, (row % 2 + 1) * half))
        field[at + row, PAD : PAD + half] = up_2[piece]
        field[at + 2 * block + row, PAD : PAD + half] = down_2[piece]


def coarse_scratch(rows, width, depth, fields):
    padded = pltpu.VMEM((rows, width + 2 * PAD, depth), jnp.float32)
    plain = pltpu.VMEM((rows, width, depth), jnp.float32)
    return [padded] * fields + [padded, plain, padded, plain, plain]


def phase_three_kernel(
    slabs, where, up_1, down_1, up_2, down_2, up_3, down_3, second, initial, kappa,
    source, kappa_c, second_near, third_out, tau_out, cross_out, *scratch,
):
    state, other = scratch[:2]
    base, spare, kappa_wide, *weights = scratch[7:14]
    pair = scratch[14]
    rows, width = kappa.shape[:2]
    block, half = kappa_c.shape[:2]
    clear_edges(state)
    fill(state, [(up_3, 0, STEPS, 0), (down_3, 0, STEPS, STEPS + rows)])

    @pl.when(where[0] == 13)
    def _():
        fill(state, [(initial, 0, rows, STEPS)])

    @pl.when(where[0] != 13)
    def _():
        fill(state, [(second, 0, rows, STEPS)])

    clear_edges(base)
    for row in range(block + 2):
        fine_row = STEPS - 2 + 2 * row
        pair[...] = (
            state[fine_row, PAD : PAD + width] + state[fine_row + 1, PAD : PAD + width]
        )
        base[row, PAD : PAD + half] = 0.25 * (
            pair[pl.ds(0, half, stride=2), :] + pair[pl.ds(1, half, stride=2), :]
        )

    def out(rows, value):
        third_out[rows] = value

    four_steps(where, slabs, up_1, down_1, kappa, source, scratch, out)

    @pl.when(lax.rem(where[0], GROUP) < 2)
    def _():
        cross_out[...] = second_near[...]

    @pl.when(lax.rem(where[0], GROUP) >= 2)
    def _():
        cross_out[...] = third_out[...]

    coarse_kappa_4(kappa_wide, up_2, down_2, kappa_c, 0)
    face_weights(kappa_wide, weights, 4.0 * ALONG_THIRD)

    def keep(rows, value):
        tau_out[rows] = value

    sweep(base, spare, weights, None, 1, block, block - 1, lambda row: (0, None), keep)
    use = jnp.where(where[0] == 13, 0.0, 1.0)
    for row in range(block):
        pair[...] = third_out[2 * row] + third_out[2 * row + 1]
        now = 0.25 * (
            pair[pl.ds(0, half, stride=2), :] + pair[pl.ds(1, half, stride=2), :]
        )
        tau_out[row] = now - use * tau_out[row]


def coarse_kappa_8(field, up_2, down_2, up_3, down_3, kappa_c):
    block, half = kappa_c.shape[:2]
    coarse_kappa_4(field, up_2, down_2, kappa_c, block)
    for row in range(block):
        piece = (STEPS + row // 2, slice(row % 2 * half, (row % 2 + 1) * half))
        field[row, PAD : PAD + half] = up_3[piece]
        field[4 * block + row, PAD : PAD + half] = down_3[piece]


def far_sums_kernel(
    slabs, where, got_a, got_b, wide_a, wide_b, up_2, down_2, up_3, down_3, kappa_c,
    ahead_out, wrapped_out, ahead_2, wrapped_2, ahead_1, wrapped_1, *scratch,
):
    field, spare, kappa_wide, *weights = scratch
    block = kappa_c.shape[0]
    deep = 2 * block - 1
    rows = block + 2 * deep
    part = rows // 2
    local = lax.rem(where[0], GROUP)
    high = where[0] >= GROUP
    clear_edges(field)
    clear_edges(spare)
    coarse_kappa_8(kappa_wide, up_2, down_2, up_3, down_3, kappa_c)
    face_weights(kappa_wide, weights, 4.0 * ALONG_THIRD)
    fill(field, [(got_a, 1, part, 0), (got_b, 0, part, part)])
    inside = inside_of(where[1], slabs, deep, block)
    late = local >= 4
    to_ahead = jnp.where(late & ~(high & (local >= 5)), 1.0, 0.0)
    to_wrapped = jnp.where(late | (high & (local == 0)), 0.0, 1.0)

    def out(rows, value):
        ahead_out[rows] = to_ahead * value
        wrapped_out[rows] = to_wrapped * value

    src, dst = field, spare
    for step in range(1, block + 1):
        sweep(
            src, dst, weights, None, step, rows - 2 * step, 1, inside,
            out if step == block else None,
        )
        src, dst = dst, src
    cut = part - block
    ahead_out[:cut] = ahead_out[:cut] + wide_a[block + 1 :]
    ahead_out[cut:] = ahead_out[cut:] + wide_b[: rows - 2 * block - cut]
    for full, two, one in (
        (ahead_out, ahead_2, ahead_1),
        (wrapped_out, wrapped_2, wrapped_1),
    ):
        two[...] = full[1:-1]
        one[...] = full[2:-2]


def near_sums_kernel(
    slabs, where, got_3, got_2, got_1, behind_3, behind_2, behind_1, own_ahead,
    own_wrapped, up_2, down_2, kappa_c, ahead_out, wrapped_out, last_out, *scratch,
):
    ahead, wrapped, spare, kappa_wide, *weights = scratch
    block, half = kappa_c.shape[:2]
    local = lax.rem(where[0], GROUP)
    high = where[0] >= GROUP
    for field in (ahead, wrapped, spare):
        clear_edges(field)
    coarse_kappa_4(kappa_wide, up_2, down_2, kappa_c, 0)
    face_weights(kappa_wide, weights, 4.0 * ALONG_THIRD)
    inside = inside_of(where[1], slabs, block, block)
    own = slice(block - 1, 2 * block - 1)
    for is_ahead in (True, False):
        src, dst = (ahead, spare) if is_ahead else (wrapped, spare)
        for distance, got, behind in (
            (3, got_3, behind_3), (2, got_2, behind_2), (1, got_1, behind_1),
        ):
            apart = high & (local >= 5) & (local < distance + 5)
            use = (local >= distance) & ~apart if is_ahead else local < distance
            value = jnp.where(use, 1.0, 0.0) * got[...]
            if not is_ahead:
                value = value + behind[...]
            at = (
                slice(block - distance, 2 * block + distance),
                slice(PAD, PAD + half),
            )
            src[at] = value if distance == 3 else src[at] + value
            if distance == 1:

                def out(rows, value, is_ahead=is_ahead):
                    result, mine = (
                        (ahead_out, own_ahead) if is_ahead else (wrapped_out, own_wrapped)
                    )
                    result[rows] = value + mine[own][rows]

            else:
                out = None
            sweep(
                src, dst, weights, None, block - distance + 1, block + 2 * distance - 2,
                0, inside, out,
            )
            src, dst = dst, src
    hand_wrapped = high & (local < 5)

    @pl.when(hand_wrapped)
    def _():
        last_out[...] = wrapped_out[...]

    @pl.when(jnp.logical_not(hand_wrapped))
    def _():
        last_out[...] = ahead_out[...]


def hand_over_kernel(
    slabs, where, far_up, near_up, last, near_down, far_down, up_2, down_2, up_3, down_3,
    kappa_c, ahead, wrapped, _, handed_out, kept_out, *scratch,
):
    field, spare, kappa_wide, *weights = scratch
    block, half = kappa_c.shape[:2]
    local = lax.rem(where[0], GROUP)
    high = where[0] >= GROUP
    clear_edges(field)
    clear_edges(spare)
    coarse_kappa_8(kappa_wide, up_2, down_2, up_3, down_3, kappa_c)
    fill(
        field,
        [
            (far_up, 0, block, 0),
            (near_up, 0, block, block),
            (last, 0, block, 2 * block),
            (near_down, 0, block, 3 * block),
            (far_down, 0, block, 4 * block),
        ],
    )
    face_weights(kappa_wide, weights, 4.0 * ALONG_THIRD)
    inside = inside_of(where[1], slabs, 2 * block, block)
    early = local < 5

    def one(use):
        return jnp.where(use, 1.0, 0.0)

    hand_image = one(early & ~high)
    hand_wrapped = one(early)
    hand_ahead = one(~early)
    keep_image = one(high)
    keep_wrapped = one(high & ~early)
    keep_ahead = one(early)

    def out(rows, value):
        a, w = ahead[rows], wrapped[rows]
        handed_out[rows] = hand_image * value + hand_wrapped * w + hand_ahead * a
        kept_out[rows] = keep_image * value + keep_wrapped * w + keep_ahead * a

    src, dst = field, spare
    for step in range(1, 2 * block + 1):
        count = 5 * block - 2 * step
        sweep(
            src, dst, weights, None, step, count, 0, inside,
            out if step == 2 * block else None,
        )
        src, dst = dst, src


def call(kernel, slabs, outs, scratch, where, *args, unread=0, room=40):
    vmem = pl.BlockSpec(memory_space=pltpu.VMEM)
    anywhere = pl.BlockSpec(memory_space=pl.ANY)
    return pl.pallas_call(
        kernel if slabs is None else functools.partial(kernel, slabs),
        out_shape=[jax.ShapeDtypeStruct(shape, jnp.float32) for shape in outs],
        in_specs=[pl.BlockSpec(memory_space=pltpu.SMEM)]
        + [vmem] * (len(args) - unread)
        + [anywhere] * unread,
        out_specs=[vmem] * len(outs),
        scratch_shapes=scratch,
        compiler_params=pltpu.CompilerParams(vmem_limit_bytes=room * 2**20),
        cost_estimate=pl.CostEstimate(flops=0, bytes_accessed=0, transcendentals=0),
    )(where, *args)


def per_device(initial, guess, conductivity, source):
    rows, width_two, width_three = conductivity.shape
    crows, half = rows // 2, width_two // 2
    slabs = lax.axis_size("space")
    tm = lax.axis_index("tm")
    sp = lax.axis_index("space")
    local = tm % GROUP
    where = jnp.stack([tm, sp]).astype(jnp.int32)

    def along_space(block, distance):
        pairs = [
            (i, i + distance) for i in range(slabs) if 0 <= i + distance < slabs
        ]
        return lax.ppermute(block, "space", pairs)

    def along_time(block, pairs):
        return lax.ppermute(block, "tm", pairs)

    def ring(shift):
        return [
            (g * GROUP + i, g * GROUP + (i + shift) % GROUP)
            for g in (0, 1)
            for i in range(GROUP)
        ]

    def restrict(field):
        return field.reshape(-1, 2, half, 2, width_three).mean(axis=(1, 3))

    def neighbours(block_first, block_last):
        return along_space(block_last, 1), along_space(block_first, -1)

    block_shape = (rows, width_two, width_three)
    coarse_shape = (crows, half, width_three)
    packed_shape = (STEPS + crows // 2, width_two, width_three)
    scratch = fine_scratch(rows, width_two, width_three)

    kappa_c = restrict(conductivity)
    first, last = call(
        first_ends_kernel, None, [(3 * STEPS - 1, width_two, width_three)] * 2,
        [pltpu.SemaphoreType.DMA((6,))],
        where, guess[0], initial, conductivity, source, unread=4, room=60,
    )
    sides = neighbours(first, last)
    state, first, last = call(
        phase_one_kernel, slabs, [block_shape, packed_shape, packed_shape], scratch,
        where, *sides, guess[0], initial, conductivity, source, kappa_c,
    )
    sides_2 = neighbours(first, last)
    second, first, last = call(
        phase_two_kernel, slabs, [block_shape, packed_shape, packed_shape], scratch,
        where, *sides, *sides_2, state, initial, conductivity, source,
    )
    sides_3 = neighbours(first, last)
    second_near = along_time(second, ring(2))
    third, tau, crossed = call(
        phase_three_kernel, slabs, [block_shape, coarse_shape, block_shape],
        scratch
        + coarse_scratch(3 * crows, half, width_three, 2)
        + [pltpu.VMEM((width_two, width_three), jnp.float32)],
        where, *sides, *sides_2, *sides_3, second, initial, conductivity, source, kappa_c,
        second_near,
    )

    far = (along_space(tau, 2), along_space(tau, -2))
    near = neighbours(tau, tau)
    tau_wide = jnp.concatenate([far[0], near[0], tau, near[1], far[1]], 0)
    part = tau_wide.shape[0] // 2
    wide = (tau_wide[:part], tau_wide[part:])
    got_a = along_time(wide[0], ring(4))
    crossed = along_time(
        lax.optimization_barrier((crossed, got_a))[0],
        [(i, i ^ GROUP) for i in range(2 * GROUP) if i % GROUP in (0, 1, 5, 6, 7)],
    )
    got_b = along_time(wide[1], ring(4))
    ahead, wrapped, *narrow = call(
        far_sums_kernel, slabs,
        [
            (crows + 2 * d,) + coarse_shape[1:] for d in (3, 2, 1) for _ in range(2)
        ],
        coarse_scratch(5 * crows, half, width_three, 2),
        where, got_a, got_b, *wide, *sides_2, *sides_3, kappa_c,
    )
    behind_pairs = lambda d: [
        (g * GROUP + i, g * GROUP + i + d) for g in (0, 1) for i in range(4)
    ]
    sent = dict(zip((3, 2, 1), ((ahead, wrapped), narrow[:2], narrow[2:])))
    got = [along_time(sent[d][0], ring(d)) for d in (3, 2, 1)]
    behind = [along_time(sent[d][1], behind_pairs(d)) for d in (3, 2, 1)]
    ahead, wrapped, last = call(
        near_sums_kernel, slabs, [coarse_shape] * 3,
        coarse_scratch(3 * crows, half, width_three, 3),
        where, *got, *behind, ahead, wrapped, *sides_2, kappa_c,
    )

    near = neighbours(last, last)
    far = (along_space(last, 2), along_space(last, -2))
    handed, kept = call(
        hand_over_kernel, slabs, [coarse_shape] * 2,
        coarse_scratch(5 * crows, half, width_three, 2),
        where, far[0], near[0], last, near[1], far[1], *sides_2, *sides_3, kappa_c,
        ahead, wrapped, crossed, unread=1,
    )
    third = lax.optimization_barrier(
        (jnp.where(local >= 5, crossed, third), handed)
    )[0]
    handed = along_time(
        handed,
        [
            (g * GROUP + i, (1 - g) * GROUP + (i + 3) % GROUP)
            for g in (0, 1)
            for i in range(GROUP)
        ],
    )
    kept = along_time(kept, ring(3))
    third_home = along_time(third, ring(3))
    second_home = jnp.where(local < 2, crossed, second_near)

    residual = third_home - second_home
    change = handed + kept - restrict(second_home)
    finer = jnp.repeat(jnp.repeat(change, 2, axis=0), 2, axis=1)
    corrected = second_home + finer
    return (corrected[None], residual[None])


def solution(mesh):
    in_specs = (
        P("space", None, None),
        P("tm", "space", None, None),
        P("space", None, None),
        P("space", None, None),
    )
    out_specs = (P("tm", "space", None, None), P("tm", "space", None, None))
    return jax.shard_map(
        per_device, mesh=mesh, in_specs=in_specs, out_specs=out_specs, check_vma=False
    )
```

```python
import functools

import jax
import jax.numpy as jnp
from jax import lax
from jax.experimental import pallas as pl
from jax.experimental.pallas import tpu as pltpu
from jax.sharding import PartitionSpec as P

STEPS = 4
ALONG_FIRST = 0.1
ALONG_SECOND = 0.1
ALONG_THIRD = 0.0125
GROUP = 8
PAD = 8


def lane_mask(shape, *lanes):
    lane = lax.broadcasted_iota(jnp.int32, shape, 1)
    hit = lane == lanes[0]
    for other in lanes[1:]:
        hit = hit | (lane == other)
    return hit


def clear_edges(field):
    rows, wide, depth = field.shape
    zero = jnp.zeros((rows, PAD, depth), jnp.float32)
    field[:, :PAD] = zero
    field[:, wide - PAD :] = zero


def face_weights(kappa, weights, third):
    by_first, by_second, by_third, keep = weights
    rows, wide, depth = kappa.shape
    width = wide - 2 * PAD
    first_w, third_w = 0.5 * ALONG_FIRST, 0.5 * third
    inner = slice(PAD, PAD + width)
    for row in range(rows):
        k = kappa[row, inner]
        if row:
            by_first[row] = first_w * (kappa[row - 1, inner] + k)
        by_second[row, inner] = first_w * (kappa[row, PAD - 1 : PAD - 1 + width] + k)
        by_second[row, PAD + width :] = (
            first_w * kappa[row, PAD + width - 1 : 2 * PAD + width - 1]
        )
        deeper = pltpu.roll(k, depth - 1, 1)
        by_third[row] = jnp.where(
            lane_mask(k.shape, depth - 1), 0.0, third_w * (k + deeper)
        )
        keep[row] = jnp.where(lane_mask(k.shape, 0, depth - 1), 1.0 - third_w * k, 1.0)


def sweep(src, dst, weights, heat, first, count, shift, inside, out=None):
    by_first, by_second, by_third, keep = weights
    wide, depth = src.shape[1:]
    width = wide - 2 * PAD
    most = max(1, 256 // width)
    inner = slice(PAD, PAD + width)
    upper = slice(PAD + 1, PAD + 1 + width)
    lower = slice(PAD - 1, PAD - 1 + width)
    row = first
    while row < first + count:
        key, mask = inside(row)
        end = row + 1
        while end < first + count and end - row < most and inside(end)[0] == key:
            end += 1
        here = slice(row, end)
        w = slice(row + shift, end + shift)
        v = src[here, inner]
        total = by_first[row + shift + 1 : end + shift + 1] * (
            src[row + 1 : end + 1, inner] - v
        ) - by_first[w] * (v - src[row - 1 : end - 1, inner])
        total = total + (
            by_second[w, upper] * (src[here, upper] - v)
            - by_second[w, inner] * (v - src[here, lower])
        )
        deep = by_third[w] * (pltpu.roll(v, depth - 1, 2) - v)
        total = keep[w] * v + (total + (deep - pltpu.roll(deep, 1, 2)))
        if heat is not None:
            total = total + heat(row, end)
        if mask is not None:
            total = total * mask
        if out is None:
            dst[here, inner] = total
        else:
            out(slice(row - first, end - first), total)
        row = end


def inside_of(place, slabs, margin, block):
    def inside(row):
        if row < margin:
            need = (margin - row + block - 1) // block
            return -need, jnp.where(place >= need, 1.0, 0.0)
        if row >= margin + block:
            need = (row - margin) // block
            return need, jnp.where(place + need < slabs, 1.0, 0.0)
        return 0, None

    return inside


def fill(field, pieces):
    width = field.shape[1] - 2 * PAD
    for ref, first, count, row in pieces:
        field[row : row + count, PAD : PAD + width] = ref[first : first + count]


def fine_scratch(rows, width, depth):
    high = rows + 2 * STEPS
    padded = pltpu.VMEM((high, width + 2 * PAD, depth), jnp.float32)
    plain = pltpu.VMEM((high, width, depth), jnp.float32)
    return [padded, padded, padded, plain, padded, plain, plain]


def four_steps(where, slabs, up_1, down_1, kappa, source, scratch, out):
    state, other, kappa_wide = scratch[:3]
    weights = scratch[3:7]
    rows = kappa.shape[0]
    for field in (other, kappa_wide):
        clear_edges(field)
    fill(
        kappa_wide,
        [
            (up_1, STEPS, STEPS, 0),
            (kappa, 0, rows, STEPS),
            (down_1, STEPS, STEPS, STEPS + rows),
        ],
    )
    face_weights(kappa_wide, weights, ALONG_THIRD)

    def heat(row, end):
        if row < STEPS:
            return up_1[2 * STEPS + row - 1 : 2 * STEPS + end - 1]
        if row < STEPS + rows:
            return source[row - STEPS : end - STEPS]
        return down_1[STEPS + row - rows : STEPS + end - rows]

    inside = inside_of(where[1], slabs, STEPS, rows)
    src, dst = state, other
    for step in range(1, STEPS + 1):
        count = rows + 2 * (STEPS - step)
        sweep(
            src, dst, weights, heat, step, count, 0, inside, out if step == STEPS else None
        )
        src, dst = dst, src


def first_ends_kernel(
    where, guess, initial, kappa, source, first_out, last_out, sems
):
    rows = kappa.shape[0]

    def copies(state):
        index = 0
        for out, at, heat in (
            (first_out, 0, 0),
            (last_out, rows - STEPS, rows - STEPS + 1),
        ):
            for ref, first, count, row in (
                (state, at, STEPS, 0),
                (kappa, at, STEPS, STEPS),
                (source, heat, STEPS - 1, 2 * STEPS),
            ):
                yield pltpu.make_async_copy(
                    ref.at[pl.ds(first, count)], out.at[pl.ds(row, count)], sems.at[index]
                )
                index += 1

    @pl.when(where[0] == 15)
    def _():
        for copy in copies(initial):
            copy.start()
        for copy in copies(initial):
            copy.wait()

    @pl.when(where[0] != 15)
    def _():
        for copy in copies(guess):
            copy.start()
        for copy in copies(guess):
            copy.wait()


def phase_one_kernel(
    slabs, where, up_1, down_1, guess, initial, kappa, source, kappa_c,
    state_out, first_out, last_out, *scratch,
):
    state = scratch[0]
    rows = kappa.shape[0]
    clear_edges(state)
    fill(state, [(up_1, 0, STEPS, 0), (down_1, 0, STEPS, STEPS + rows)])

    @pl.when(where[0] == 15)
    def _():
        fill(state, [(initial, 0, rows, STEPS)])

    @pl.when(where[0] != 15)
    def _():
        fill(state, [(guess, 0, rows, STEPS)])

    def out(rows, value):
        state_out[rows] = value

    four_steps(where, slabs, up_1, down_1, kappa, source, scratch, out)

    @pl.when(where[0] == 14)
    def _():
        state_out[...] = initial[...]

    first_out[:STEPS] = state_out[:STEPS]
    last_out[:STEPS] = state_out[rows - STEPS :]
    half = kappa_c.shape[1]
    for row in range(rows // 2):
        at = (STEPS + row // 2, slice(row % 2 * half, (row % 2 + 1) * half))
        first_out[at] = kappa_c[row]
        last_out[at] = kappa_c[row]


def phase_two_kernel(
    slabs, where, up_1, down_1, up_2, down_2, before, initial, kappa, source,
    second_out, first_out, last_out, *scratch,
):
    state = scratch[0]
    rows = kappa.shape[0]
    clear_edges(state)
    fill(
        state,
        [
            (up_2, 0, STEPS, 0),
            (before, 0, rows, STEPS),
            (down_2, 0, STEPS, STEPS + rows),
        ],
    )

    def out(rows, value):
        second_out[rows] = value

    four_steps(where, slabs, up_1, down_1, kappa, source, scratch, out)

    @pl.when(where[0] == 13)
    def _():
        first_out[:STEPS] = initial[:STEPS]
        last_out[:STEPS] = initial[rows - STEPS :]

    @pl.when(where[0] != 13)
    def _():
        first_out[:STEPS] = second_out[:STEPS]
        last_out[:STEPS] = second_out[rows - STEPS :]

    first_out[STEPS:] = down_2[STEPS:]
    last_out[STEPS:] = up_2[STEPS:]


def coarse_kappa_4(field, up_2, down_2, kappa_c, at):
    block, half = kappa_c.shape[:2]
    clear_edges(field)
    fill(field, [(kappa_c, 0, block, at + block)])
    for row in range(block):
        piece = (STEPS + row // 2, slice(row % 2 * half, (row % 2 + 1) * half))
        field[at + row, PAD : PAD + half] = up_2[piece]
        field[at + 2 * block + row, PAD : PAD + half] = down_2[piece]


def coarse_scratch(rows, width, depth, fields):
    padded = pltpu.VMEM((rows, width + 2 * PAD, depth), jnp.float32)
    plain = pltpu.VMEM((rows, width, depth), jnp.float32)
    return [padded] * fields + [padded, plain, padded, plain, plain]


def phase_three_kernel(
    slabs, where, up_1, down_1, up_2, down_2, up_3, down_3, second, initial, kappa,
    source, kappa_c, second_near, third_out, tau_out, cross_out, *scratch,
):
    state, other = scratch[:2]
    base, spare, kappa_wide, *weights = scratch[7:14]
    pair = scratch[14]
    rows, width = kappa.shape[:2]
    block, half = kappa_c.shape[:2]
    clear_edges(state)
    fill(state, [(up_3, 0, STEPS, 0), (down_3, 0, STEPS, STEPS + rows)])

    @pl.when(where[0] == 13)
    def _():
        fill(state, [(initial, 0, rows, STEPS)])

    @pl.when(where[0] != 13)
    def _():
        fill(state, [(second, 0, rows, STEPS)])

    clear_edges(base)
    for row in range(block + 2):
        fine_row = STEPS - 2 + 2 * row
        pair[...] = (
            state[fine_row, PAD : PAD + width] + state[fine_row + 1, PAD : PAD + width]
        )
        base[row, PAD : PAD + half] = 0.25 * (
            pair[pl.ds(0, half, stride=2), :] + pair[pl.ds(1, half, stride=2), :]
        )

    def out(rows, value):
        third_out[rows] = value

    four_steps(where, slabs, up_1, down_1, kappa, source, scratch, out)

    @pl.when(lax.rem(where[0], GROUP) < 2)
    def _():
        cross_out[...] = second_near[...]

    @pl.when(lax.rem(where[0], GROUP) >= 2)
    def _():
        cross_out[...] = third_out[...]

    coarse_kappa_4(kappa_wide, up_2, down_2, kappa_c, 0)
    face_weights(kappa_wide, weights, 4.0 * ALONG_THIRD)

    def keep(rows, value):
        tau_out[rows] = value

    sweep(base, spare, weights, None, 1, block, block - 1, lambda row: (0, None), keep)
    use = jnp.where(where[0] == 13, 0.0, 1.0)
    for row in range(block):
        pair[...] = third_out[2 * row] + third_out[2 * row + 1]
        now = 0.25 * (
            pair[pl.ds(0, half, stride=2), :] + pair[pl.ds(1, half, stride=2), :]
        )
        tau_out[row] = now - use * tau_out[row]


def coarse_kappa_8(field, up_2, down_2, up_3, down_3, kappa_c):
    block, half = kappa_c.shape[:2]
    coarse_kappa_4(field, up_2, down_2, kappa_c, block)
    for row in range(block):
        piece = (STEPS + row // 2, slice(row % 2 * half, (row % 2 + 1) * half))
        field[row, PAD : PAD + half] = up_3[piece]
        field[4 * block + row, PAD : PAD + half] = down_3[piece]


def far_sums_kernel(
    slabs, where, got_a, got_b, wide_a, wide_b, up_2, down_2, up_3, down_3, kappa_c,
    ahead_out, wrapped_out, ahead_2, wrapped_2, ahead_1, wrapped_1, *scratch,
):
    field, spare, kappa_wide, *weights = scratch
    block = kappa_c.shape[0]
    deep = 2 * block - 1
    rows = block + 2 * deep
    part = got_a.shape[0] - 1
    local = lax.rem(where[0], GROUP)
    high = where[0] >= GROUP
    clear_edges(field)
    clear_edges(spare)
    coarse_kappa_8(kappa_wide, up_2, down_2, up_3, down_3, kappa_c)
    face_weights(kappa_wide, weights, 4.0 * ALONG_THIRD)
    fill(field, [(got_a, 1, part, 0), (got_b, 0, rows - part, part)])
    inside = inside_of(where[1], slabs, deep, block)
    late = local >= 4
    to_ahead = jnp.where(late & ~(high & (local >= 5)), 1.0, 0.0)
    to_wrapped = jnp.where(late | (high & (local == 0)), 0.0, 1.0)

    def out(rows, value):
        ahead_out[rows] = to_ahead * value
        wrapped_out[rows] = to_wrapped * value

    src, dst = field, spare
    for step in range(1, block + 1):
        sweep(
            src, dst, weights, None, step, rows - 2 * step, 1, inside,
            out if step == block else None,
        )
        src, dst = dst, src
    cut = part - block
    ahead_out[:cut] = ahead_out[:cut] + wide_a[block + 1 :]
    ahead_out[cut:] = ahead_out[cut:] + wide_b[: rows - 2 * block - cut]
    for full, two, one in (
        (ahead_out, ahead_2, ahead_1),
        (wrapped_out, wrapped_2, wrapped_1),
    ):
        two[...] = full[1:-1]
        one[...] = full[2:-2]


def near_sums_kernel(
    slabs, where, got_3, got_2, got_1, behind_3, behind_2, behind_1, own_ahead,
    own_wrapped, up_2, down_2, kappa_c, ahead_out, wrapped_out, last_out, *scratch,
):
    ahead, wrapped, spare, kappa_wide, *weights = scratch
    block, half = kappa_c.shape[:2]
    local = lax.rem(where[0], GROUP)
    high = where[0] >= GROUP
    for field in (ahead, wrapped, spare):
        clear_edges(field)
    coarse_kappa_4(kappa_wide, up_2, down_2, kappa_c, 0)
    face_weights(kappa_wide, weights, 4.0 * ALONG_THIRD)
    inside = inside_of(where[1], slabs, block, block)
    own = slice(block - 1, 2 * block - 1)
    for is_ahead in (True, False):
        src, dst = (ahead, spare) if is_ahead else (wrapped, spare)
        for distance, got, behind in (
            (3, got_3, behind_3), (2, got_2, behind_2), (1, got_1, behind_1),
        ):
            apart = high & (local >= 5) & (local < distance + 5)
            use = (local >= distance) & ~apart if is_ahead else local < distance
            value = jnp.where(use, 1.0, 0.0) * got[...]
            if not is_ahead:
                value = value + behind[...]
            at = (
                slice(block - distance, 2 * block + distance),
                slice(PAD, PAD + half),
            )
            src[at] = value if distance == 3 else src[at] + value
            if distance == 1:

                def out(rows, value, is_ahead=is_ahead):
                    result, mine = (
                        (ahead_out, own_ahead) if is_ahead else (wrapped_out, own_wrapped)
                    )
                    result[rows] = value + mine[own][rows]

            else:
                out = None
            sweep(
                src, dst, weights, None, block - distance + 1, block + 2 * distance - 2,
                0, inside, out,
            )
            src, dst = dst, src
    hand_wrapped = high & (local < 5)

    @pl.when(hand_wrapped)
    def _():
        last_out[...] = wrapped_out[...]

    @pl.when(jnp.logical_not(hand_wrapped))
    def _():
        last_out[...] = ahead_out[...]


def hand_over_kernel(
    slabs, where, far_up, near_up, last, near_down, far_down, up_2, down_2, up_3, down_3,
    kappa_c, ahead, wrapped, _, handed_out, kept_out, *scratch,
):
    field, spare, kappa_wide, *weights = scratch
    block, half = kappa_c.shape[:2]
    local = lax.rem(where[0], GROUP)
    high = where[0] >= GROUP
    clear_edges(field)
    clear_edges(spare)
    coarse_kappa_8(kappa_wide, up_2, down_2, up_3, down_3, kappa_c)
    fill(
        field,
        [
            (far_up, 0, block, 0),
            (near_up, 0, block, block),
            (last, 0, block, 2 * block),
            (near_down, 0, block, 3 * block),
            (far_down, 0, block, 4 * block),
        ],
    )
    face_weights(kappa_wide, weights, 4.0 * ALONG_THIRD)
    inside = inside_of(where[1], slabs, 2 * block, block)
    early = local < 5

    def one(use):
        return jnp.where(use, 1.0, 0.0)

    hand_image = one(early & ~high)
    hand_wrapped = one(early)
    hand_ahead = one(~early)
    keep_image = one(high)
    keep_wrapped = one(high & ~early)
    keep_ahead = one(early)

    def out(rows, value):
        a, w = ahead[rows], wrapped[rows]
        handed_out[rows] = hand_image * value + hand_wrapped * w + hand_ahead * a
        kept_out[rows] = keep_image * value + keep_wrapped * w + keep_ahead * a

    src, dst = field, spare
    for step in range(1, 2 * block + 1):
        count = 5 * block - 2 * step
        sweep(
            src, dst, weights, None, step, count, 0, inside,
            out if step == 2 * block else None,
        )
        src, dst = dst, src


def call(kernel, slabs, outs, scratch, where, *args, unread=0, room=40):
    vmem = pl.BlockSpec(memory_space=pltpu.VMEM)
    anywhere = pl.BlockSpec(memory_space=pl.ANY)
    return pl.pallas_call(
        kernel if slabs is None else functools.partial(kernel, slabs),
        out_shape=[jax.ShapeDtypeStruct(shape, jnp.float32) for shape in outs],
        in_specs=[pl.BlockSpec(memory_space=pltpu.SMEM)]
        + [vmem] * (len(args) - unread)
        + [anywhere] * unread,
        out_specs=[vmem] * len(outs),
        scratch_shapes=scratch,
        compiler_params=pltpu.CompilerParams(vmem_limit_bytes=room * 2**20),
        cost_estimate=pl.CostEstimate(flops=0, bytes_accessed=0, transcendentals=0),
    )(where, *args)


def per_device(initial, guess, conductivity, source):
    rows, width_two, width_three = conductivity.shape
    crows, half = rows // 2, width_two // 2
    slabs = lax.axis_size("space")
    tm = lax.axis_index("tm")
    sp = lax.axis_index("space")
    local = tm % GROUP
    where = jnp.stack([tm, sp]).astype(jnp.int32)

    def along_space(block, distance):
        pairs = [
            (i, i + distance) for i in range(slabs) if 0 <= i + distance < slabs
        ]
        return lax.ppermute(block, "space", pairs)

    def along_time(block, pairs):
        return lax.ppermute(block, "tm", pairs)

    def ring(shift):
        return [
            (g * GROUP + i, g * GROUP + (i + shift) % GROUP)
            for g in (0, 1)
            for i in range(GROUP)
        ]

    def restrict(field):
        return field.reshape(-1, 2, half, 2, width_three).mean(axis=(1, 3))

    def neighbours(block_first, block_last):
        return along_space(block_last, 1), along_space(block_first, -1)

    block_shape = (rows, width_two, width_three)
    coarse_shape = (crows, half, width_three)
    packed_shape = (STEPS + crows // 2, width_two, width_three)
    scratch = fine_scratch(rows, width_two, width_three)

    kappa_c = restrict(conductivity)
    first, last = call(
        first_ends_kernel, None, [(3 * STEPS - 1, width_two, width_three)] * 2,
        [pltpu.SemaphoreType.DMA((6,))],
        where, guess[0], initial, conductivity, source, unread=4, room=60,
    )
    sides = neighbours(first, last)
    state, first, last = call(
        phase_one_kernel, slabs, [block_shape, packed_shape, packed_shape], scratch,
        where, *sides, guess[0], initial, conductivity, source, kappa_c,
    )
    sides_2 = neighbours(first, last)
    second, first, last = call(
        phase_two_kernel, slabs, [block_shape, packed_shape, packed_shape], scratch,
        where, *sides, *sides_2, state, initial, conductivity, source,
    )
    sides_3 = neighbours(first, last)
    second_near = along_time(second, ring(2))
    third, tau, crossed = call(
        phase_three_kernel, slabs, [block_shape, coarse_shape, block_shape],
        scratch
        + coarse_scratch(3 * crows, half, width_three, 2)
        + [pltpu.VMEM((width_two, width_three), jnp.float32)],
        where, *sides, *sides_2, *sides_3, second, initial, conductivity, source, kappa_c,
        second_near,
    )

    far = (along_space(tau, 2), along_space(tau, -2))
    near = neighbours(tau, tau)
    tau_wide = jnp.concatenate([far[0], near[0], tau, near[1], far[1]], 0)
    part = crows + 2
    wide = (tau_wide[:part], tau_wide[part:])
    got_a = along_time(wide[0], ring(4))
    crossed = along_time(
        lax.optimization_barrier((crossed, got_a))[0],
        [(i, i ^ GROUP) for i in range(2 * GROUP) if i % GROUP in (0, 1, 5, 6, 7)],
    )
    got_b = along_time(wide[1], ring(4))
    ahead, wrapped, *narrow = call(
        far_sums_kernel, slabs,
        [
            (crows + 2 * d,) + coarse_shape[1:] for d in (3, 2, 1) for _ in range(2)
        ],
        coarse_scratch(5 * crows, half, width_three, 2),
        where, got_a, got_b, *wide, *sides_2, *sides_3, kappa_c,
    )
    behind_pairs = lambda d: [
        (g * GROUP + i, g * GROUP + i + d) for g in (0, 1) for i in range(4)
    ]
    sent = dict(zip((3, 2, 1), ((ahead, wrapped), narrow[:2], narrow[2:])))
    got = [along_time(sent[d][0], ring(d)) for d in (3, 2, 1)]
    behind = [along_time(sent[d][1], behind_pairs(d)) for d in (3, 2, 1)]
    ahead, wrapped, last = call(
        near_sums_kernel, slabs, [coarse_shape] * 3,
        coarse_scratch(3 * crows, half, width_three, 3),
        where, *got, *behind, ahead, wrapped, *sides_2, kappa_c,
    )

    near = neighbours(last, last)
    far = (along_space(last, 2), along_space(last, -2))
    handed, kept = call(
        hand_over_kernel, slabs, [coarse_shape] * 2,
        coarse_scratch(5 * crows, half, width_three, 2),
        where, far[0], near[0], last, near[1], far[1], *sides_2, *sides_3, kappa_c,
        ahead, wrapped, crossed, unread=1,
    )
    third = lax.optimization_barrier(
        (jnp.where(local >= 5, crossed, third), handed)
    )[0]
    handed = along_time(
        handed,
        [
            (g * GROUP + i, (1 - g) * GROUP + (i + 3) % GROUP)
            for g in (0, 1)
            for i in range(GROUP)
        ],
    )
    kept = along_time(kept, ring(3))
    third_home = along_time(third, ring(3))
    second_home = jnp.where(local < 2, crossed, second_near)

    residual = third_home - second_home
    change = handed + kept - restrict(second_home)
    finer = jnp.repeat(jnp.repeat(change, 2, axis=0), 2, axis=1)
    corrected = second_home + finer
    return (corrected[None], residual[None])


def solution(mesh):
    in_specs = (
        P("space", None, None),
        P("tm", "space", None, None),
        P("space", None, None),
        P("space", None, None),
    )
    out_specs = (P("tm", "space", None, None), P("tm", "space", None, None))
    return jax.shard_map(
        per_device, mesh=mesh, in_specs=in_specs, out_specs=out_specs, check_vma=False
    )
```
